32 devices in a mesh: fsdp: 2 (over y), heads: 4 (over z), tensor: 4 (over x, core).
Axes of the slice: x: 2, y: 2, z: 4, core: 2. Of those that a mesh axis runs over, the one named last changes fastest.
Arguments:
- tokens: bfloat16 [2048, 2048], P('fsdp'), may hold values from -6 to 6
- attn_qkv: float32 [2048, 3, 2048], P('fsdp', None, ('heads', 'tensor')), may hold values from -0.125 to 0.125
- attn_out: float32 [2048, 2048], P('fsdp', ('heads', 'tensor')), may hold values from -0.5 to 0.5
- norm_gains: float32 [2, 2048], P(None, 'fsdp'), may hold values from 0.5 to 1.5
- expert_in: float32 [2048, 2, 16, 1024], P('fsdp', None, 'heads', 'tensor'), may hold values from -0.125 to 0.125
- expert_out: float32 [2048, 16, 1024], P('fsdp', 'heads', 'tensor'), may hold values from -0.375 to 0.375
- segment_ids: int32 [2048], P('fsdp'), may hold values from 0 to 15, never falling along the last dimension, each value on 1 to 1024 neighbouring positions
- keep_mask: int32 [2048], P('fsdp'), may hold values 0 or 1
- routes: int32 [2048, 8], P('fsdp'), may hold values from 0 to 15, all different within a row; in each aligned block of 1024 rows (0 to 1023, 1024 to 2047, ...) at most 640 rows name the same one
- gate_weights: float32 [2048, 8], P('fsdp'), may hold values from 0.1 to 0.5
- cotangent: bfloat16 [2048, 2048], P('fsdp'), may hold values from -6 to 6
Outputs:
- output: bfloat16 [2048, 2048], P('fsdp')
- input_grad: float32 [2048, 2048], P('fsdp')
- qkv_grad: float32 [2048, 3, 2048], P('fsdp', None, ('heads', 'tensor'))
- out_grad: float32 [2048, 2048], P('fsdp', ('heads', 'tensor'))
- gains_grad: float32 [2, 2048], P(None, 'fsdp')
- expert_in_grad: float32 [2048, 2, 16, 1024], P('fsdp', None, 'heads', 'tensor')
- expert_out_grad: float32 [2048, 16, 1024], P('fsdp', 'heads', 'tensor')
The draws below stay inside these ranges and needn't reach their ends.
Inputs may be any that keep to these rules, and one draw needn't show every extreme that they name: `routes`: each token names 8 different experts; among the rows of one device (1024 tokens) no expert is named more than 640 times, a bound that some block reaches. `segment_ids`: never falling along the tokens; each document holds 1 to 1024 positions, one exactly 1024.
All inputs are finite; a program needn't handle non-finite values. No bound on the sum of `keep_mask` on one device may be relied on, other than what follows from the above.
Results may differ from the reference program's by a relative error of at most 0.014.
The reference program's roundings to bfloat16 on the way count: a program that leaves them out, or rounds other values in their place, can miss the bound.
Values may be sent and summed in bfloat16 or wider, within the bound.
No kernel may reach another device: no remote copies, remote signals or barrier semaphores. Data moves between devices by JAX's collectives and lax.ppermute only.
A program may use at most 320 MiB of HBM per device.

```python
import math
import jax
import jax.numpy as jnp
import numpy as np
from jax import lax

D = 2048
HEADS = 16
HEAD_DIM = 128
FF = 1024
TOPK = 8
SEQ_LEN = 1024
TOK_DEV = 1024
TOKENS = 2048
EXPERTS = 16
CAP = 640
DOCS = 16


def place_ends(result, stream_key, low, top_value):
    longest = result.shape.index(max(result.shape))
    spots = []
    for shift in (0, 1):
        where = [jax.random.randint(jax.random.fold_in(stream_key, axis), (), 0, length) for axis, length in enumerate(result.shape)]
        where[longest] = (where[longest] + shift) % result.shape[longest]
        spots.append(tuple(where))
    return result.at[spots[0]].set(low).at[spots[1]].set(top_value)


def shard_levels(stream_key, dims, shards, smallest, largest):
    loudness = 1.0
    for position, blocks in shards:
        draws = jax.random.uniform(jax.random.fold_in(jax.random.fold_in(stream_key, 6), position), (blocks,), jnp.float32, smallest / len(shards), largest / len(shards))
        loudness = loudness * jnp.repeat(jnp.exp(draws), dims[position] // blocks).reshape((-1,) + (1,) * (len(dims) - 1 - position))
    return loudness


def split_up(count, total, reach, slope):
    weights = [(1 << 20) // math.isqrt(grade ** slope) + 1 for grade in range(2, count + 1)]
    rest, holding = total - reach - (count - 1), [1] * (count - 1)
    while rest > 0:
        movable = [i for i in range(count - 1) if holding[i] < reach]
        pool, budget = sum([weights[i] for i in movable]), rest
        for i in movable:
            extra = min(reach - holding[i], max(1, budget * weights[i] // pool), rest)
            holding[i] = holding[i] + extra
            rest = rest - extra
    return np.array([reach] + holding)


def uneven(stream_key, number_of, total, bound, skew):
    if number_of == 2:
        one = jax.random.randint(stream_key, (), max(1, total - bound), min(bound, total - 1) + 1)
        return jnp.stack([one, total - one])
    sizes = jnp.asarray(split_up(number_of, total, bound, skew), jnp.int32)
    pairs = (number_of - 1) // 2
    source_of, receiver = sizes[1:1 + 2 * pairs:2], sizes[2:2 + 2 * pairs:2]
    margin = jnp.minimum(source_of - 1, bound - receiver)
    shifted = jax.random.randint(jax.random.fold_in(stream_key, 1), (pairs,), 0, 1 << 20) % (margin + 1)
    sizes = sizes.at[1:1 + 2 * pairs:2].set(source_of - shifted).at[2:2 + 2 * pairs:2].set(receiver + shifted)
    return sizes[jax.random.permutation(jax.random.fold_in(stream_key, 2), number_of)]


def shared_out(rng, own, number, rows, number_of, top, most, slope):
    order = jax.random.permutation(rng, number_of)
    heavy_load, common = load_shares(number_of, rows * top, most, slope, True), load_shares(number_of, rows * top, most, slope, False)
    places = jnp.arange(number_of)

    def named(tallies, rotation):
        used = int((tallies > 0).sum())
        fixed = max(1, used // 4)
        shifted = fixed + (places - fixed + rotation * (used - fixed)) % max(1, number_of - fixed)
        return jnp.zeros((number_of,), jnp.int32).at[order[jnp.where(places < fixed, places, shifted)]].set(jnp.asarray(tallies, jnp.int32))

    tallies = jnp.where(number % 4 == 0, named(heavy_load, number // 4), named(common, number - number // 4 - 1))
    mixed = jax.random.permutation(jax.random.fold_in(own, 3), number_of)
    donor, sink = mixed[0:number_of // 2 * 2:2], mixed[1:number_of // 2 * 2:2]
    room = jnp.minimum(tallies[donor] - 1, most - tallies[sink]) // 2
    room = jnp.where((donor == order[0]) | (sink == order[0]) | (tallies[sink] == 0), 0, jnp.maximum(room, 0))
    shifted = jax.random.randint(jax.random.fold_in(own, 4), (number_of // 2,), 0, 1 << 20) % (room + 1)
    tallies = tallies.at[donor].add(-shifted).at[sink].add(shifted)
    items = jnp.searchsorted(jnp.cumsum(tallies), jnp.arange(rows * top), side="right").astype(jnp.int32)
    grid = items.reshape(top, rows).T
    grid = grid[jax.random.permutation(jax.random.fold_in(own, 1), rows)]
    rotation = jax.random.randint(jax.random.fold_in(own, 2), (rows, 1), 0, top)
    return jnp.take_along_axis(grid, (jnp.arange(top)[None, :] + rotation) % top, axis=1)


def load_shares(number_of, total, limit, lean, full):
    portions = [(1 << 20) // math.isqrt(standing ** lean) + 1 for standing in range(1, number_of + 1)]
    largest = limit if full else min(limit, max(-(-total // number_of), total * portions[0] // sum(portions)))
    least = 1 if total - largest >= number_of - 1 else 0
    counts, spare = [largest] + [least] * (number_of - 1), total - largest - least * (number_of - 1)
    while spare > 0:
        candidates = [i for i in range(1, number_of) if counts[i] < largest] or [i for i in range(1, number_of) if counts[i] < limit]
        mass, remaining = sum([portions[i] for i in candidates]), spare
        for i in candidates:
            addition = min(limit - counts[i], max(1, remaining * portions[i] // mass), spare)
            counts[i] = counts[i] + addition
            spare = spare - addition
    return np.array(counts)


def centred(key, dims, scale, bound, cuts=(), held_as=jnp.bfloat16):
    entries = scale * jax.random.normal(key, dims, jnp.float32)
    if cuts:
        entries = entries * shard_levels(key, dims, cuts, -0.22, 0.18)
    return jnp.clip(entries, -bound, bound).astype(held_as)


def setup_inputs(seed: int = 0) -> dict:
    seeds = jax.random.split(jax.random.key(seed), 12)
    tokens = centred(seeds[0], (TOKENS, D), 1.0, 6.0, ((0, 2),))
    attn_qkv = centred(seeds[1], (D, 3, D), D ** -0.5, 0.125, ((0, 2), (2, 16)), jnp.float32)
    attn_out = centred(seeds[2], (D, D), (D // 16) ** -0.5, 0.5, ((0, 2), (1, 16)), jnp.float32)
    norm_gains = jnp.clip(1.0 + 0.1 * jax.random.normal(seeds[3], (2, D), jnp.float32), 0.5, 1.5)
    expert_in = centred(seeds[4], (D, 2, EXPERTS, FF), D ** -0.5, 0.125, ((0, 2), (2, 4), (3, 4)), jnp.float32)
    expert_out = centred(seeds[5], (D, EXPERTS, FF), (FF // 4) ** -0.5, 0.375, ((0, 2), (1, 4), (2, 4)), jnp.float32)
    segment_ids = jnp.searchsorted(jnp.cumsum(uneven(seeds[6], DOCS, TOKENS, SEQ_LEN, 2)), jnp.arange(TOKENS), side="right").astype(jnp.int32)
    keep_mask = place_ends((jax.random.randint(seeds[7], (TOKENS,), 0, 8) < 7).astype(jnp.int32), jax.random.fold_in(seeds[7], 1), 0, 1)
    routes_keys = jax.random.split(jax.random.fold_in(seeds[8], 1), TOKENS // TOK_DEV)
    routes_turns = jax.random.permutation(jax.random.fold_in(seeds[8], 3), TOKENS // TOK_DEV)
    routes = jax.vmap(lambda own, number: shared_out(jax.random.fold_in(seeds[8], 2), own, number, TOK_DEV, EXPERTS, TOPK, CAP, 1))(routes_keys, routes_turns).reshape((TOKENS, TOPK))
    gate_weights = jnp.clip(jnp.exp(math.log(0.5) - 1.609438 * jax.random.uniform(seeds[9], (TOKENS, TOPK), jnp.float32) ** shard_levels(seeds[9], (TOKENS, TOPK), ((0, 2),), -0.2, 0.2)), 0.1, 0.5)
    cotangent = centred(seeds[10], (TOKENS, D), 1.0, 6.0, ((0, 2),))
    return {"tokens": tokens, "attn_qkv": attn_qkv, "attn_out": attn_out, "norm_gains": norm_gains, "expert_in": expert_in, "expert_out": expert_out, "segment_ids": segment_ids, "keep_mask": keep_mask, "routes": routes, "gate_weights": gate_weights, "cotangent": cotangent}


@jax.custom_vjp
def low(v):
    return lax.optimization_barrier(v.astype(jnp.bfloat16)).astype(jnp.float32)

@jax.custom_vjp
def low_back(v):
    return v

def low_keep(v):
    return (low(v), None)

def low_pass(kept, grad):
    return (grad,)

def back_keep(v):
    return (v, None)

def back_low(kept, grad):
    return (low(grad),)
low.defvjp(low_keep, low_pass)
low_back.defvjp(back_keep, back_low)
epsilon = 1e-06
highest = lax.Precision.HIGHEST

def norm_gain(values, gain_row):
    return values * lax.rsqrt(lax.optimization_barrier(jnp.mean(values * values, axis=-1, keepdims=True)) + epsilon) * gain_row

def slot_positions(route_rows, expert_count, capacity):
    flat_routes = route_rows.reshape(-1).astype(jnp.int32)
    one_hot = (flat_routes[:, None] == jnp.arange(expert_count, dtype=jnp.int32)[None, :]).astype(jnp.int32)
    running = jnp.cumsum(one_hot, axis=0)
    slot_rank = lax.optimization_barrier(jnp.sum(one_hot * running, axis=1)) - 1
    return (flat_routes * capacity + slot_rank).astype(jnp.int32)

def block_forward(weights, inputs):
    qkv_weight, out_weight, gain_rows, weight_in, weight_out = weights
    block_tokens, block_segments, block_keep, block_routes, block_gates = inputs
    tok_count = block_tokens.shape[0]
    seq_count = tok_count // SEQ_LEN
    normed_one = low(norm_gain(block_tokens, gain_rows[0]))
    projected = jnp.einsum('td,dcj->ctj', normed_one, qkv_weight, precision=highest)
    projected = low(low_back(projected))
    heads_view = projected.reshape(3, seq_count, SEQ_LEN, HEADS, HEAD_DIM)
    scores = jnp.einsum('sqhe,skhe->shqk', heads_view[0], heads_view[1], precision=highest) * HEAD_DIM ** (-0.5)
    seg_grid = block_segments.reshape(seq_count, SEQ_LEN)
    keep_grid = block_keep.reshape(seq_count, SEQ_LEN)
    diagonal = jnp.arange(SEQ_LEN)[:, None] == jnp.arange(SEQ_LEN)[None, :]
    allowed = (seg_grid[:, :, None] == seg_grid[:, None, :]) & ((keep_grid[:, None, :] == 1) | diagonal[None])
    scores = low_back(jnp.where(allowed[:, None], scores, -1e+30))
    attn_probs = jax.nn.softmax(scores, axis=-1)
    attended = jnp.einsum('shqk,skhe->sqhe', low(attn_probs), heads_view[2], precision=highest)
    attended = low(low_back(attended.reshape(tok_count, D)))
    branch = low_back(jnp.einsum('tj,dj->td', attended, out_weight, precision=highest))
    middle = block_tokens + branch
    normed_two = low(norm_gain(middle, gain_rows[1]))
    positions = slot_positions(block_routes, EXPERTS, CAP)
    token_ids = jnp.arange(tok_count * TOPK, dtype=jnp.int32) // TOPK
    slot_table = jnp.zeros((EXPERTS * CAP,), jnp.int32).at[positions].set(token_ids)
    filled = jnp.zeros((EXPERTS * CAP,), jnp.float32).at[positions].set(1.0)
    slot_rows = (normed_two[slot_table] * filled[:, None]).reshape(EXPERTS, CAP, D)
    gate_up = low_back(jnp.einsum('ecd,dgef->gecf', slot_rows, weight_in, precision=highest))
    hidden = low(jax.nn.silu(gate_up[0]) * gate_up[1])
    expert_rows = low_back(jnp.einsum('ecf,def->ecd', hidden, weight_out, precision=highest))
    picked = expert_rows.reshape(EXPERTS * CAP, D)[positions].reshape(tok_count, TOPK, D)
    mixture = lax.optimization_barrier(jnp.sum(block_gates[:, :, None] * picked, axis=1))
    return middle + mixture

def reference(tokens, attn_qkv, attn_out, norm_gains, expert_in, expert_out, segment_ids, keep_mask, routes, gate_weights, cotangent):
    block_count = TOKENS // TOK_DEV
    block_step = jax.checkpoint(block_forward)

    def whole_layer(token_values, qkv_weight, out_weight, gain_rows, weight_in, weight_out):
        weights = (low(qkv_weight), low(out_weight), low(gain_rows), low(weight_in), low(weight_out))
        inputs = (token_values.reshape(block_count, TOK_DEV, D), segment_ids.reshape(block_count, TOK_DEV), keep_mask.reshape(block_count, TOK_DEV), routes.reshape(block_count, TOK_DEV, TOPK), gate_weights.reshape(block_count, TOK_DEV, TOPK))
        all_rows = lax.map(lambda block_input: block_step(weights, block_input), inputs)
        return all_rows.reshape(TOKENS, D)
    layer_out, pull_back = jax.vjp(whole_layer, tokens.astype(jnp.float32), attn_qkv, attn_out, norm_gains, expert_in, expert_out)
    gradients = pull_back(cotangent.astype(jnp.float32))
    return (layer_out.astype(jnp.bfloat16), gradients[0], gradients[1], gradients[2], gradients[3], gradients[4], gradients[5])
```

```python
import jax
import jax.numpy as jnp
from jax import lax
from jax.sharding import PartitionSpec as P

SEQ_LEN = 1024
EPS = 1e-06
BF = jnp.bfloat16
F32 = jnp.float32
GROUP = ("heads", "tensor")
EVERY = ("fsdp", "heads", "tensor")

STEPS = {
    "z1": ("heads", 2, 0),
    "z0": ("heads", 1, 1),
    "x": ("tensor", 2, 2),
    "core": ("tensor", 1, 3),
}
ORDER_A = ("core", "x", "z0", "z1")
ORDER_B = ("core", "z0", "z1", "x")


def dot(a, b, ca=1, cb=0):
    return lax.dot_general(a, b, (((ca,), (cb,)), ((), ())), preferred_element_type=F32)


def after(value, *others):
    return lax.optimization_barrier((value,) + others)[0]


def swap(v, step):
    name, bit, _ = STEPS[step]
    return lax.ppermute(v, name, [(i, i ^ bit) for i in range(lax.axis_size(name))])


def place(step):
    name, bit, dim = STEPS[step]
    return (lax.axis_index(name) // bit) % 2, dim


def reduce_rows(v, order):
    rows, cols = v.shape
    v = v.reshape(2, 2, 2, 2, rows // 16, cols)
    for step in order:
        me, dim = place(step)
        got = swap(lax.dynamic_slice_in_dim(v, 1 - me, 1, dim), step)
        mine = lax.dynamic_slice_in_dim(v, me, 1, dim)
        v = (mine.astype(F32) + got.astype(F32)).astype(BF)
    return v.reshape(rows // 16, cols)


def gather_rows(v, order):
    rows, cols = v.shape
    v = v.reshape(1, 1, 1, 1, rows, cols)
    for step in order[::-1]:
        me, dim = place(step)
        got = swap(v, step)
        shape = list(v.shape)
        shape[dim] = 2
        wide = lax.dynamic_update_slice_in_dim(jnp.zeros(shape, v.dtype), v, me, dim)
        v = lax.dynamic_update_slice_in_dim(wide, got, 1 - me, dim)
    return v.reshape(16 * rows, cols)


def reduce_pair(pair):
    return reduce_rows(pair[0].astype(BF), ORDER_A), reduce_rows(pair[1].astype(BF), ORDER_B)


def gather_pair(pair):
    return gather_rows(pair[0], ORDER_A), gather_rows(pair[1], ORDER_B)


def two_way():
    return lax.axis_size("fsdp") == 2


def across(v):
    return lax.ppermute(v, "fsdp", [(0, 1), (1, 0)])


def spread(v, axis=0):
    if two_way():
        return v, across(v)
    full = lax.all_gather(v, "fsdp", axis=axis, tiled=True)
    half = full.shape[axis] // 2
    return (
        lax.slice_in_dim(full, 0, half, axis=axis),
        lax.slice_in_dim(full, half, 2 * half, axis=axis),
    )


def halves(v):
    half = v.shape[-1] // 2
    start = lax.axis_index("fsdp") * half if two_way() else 0
    return (
        lax.dynamic_slice_in_dim(v, start, half, v.ndim - 1),
        lax.dynamic_slice_in_dim(v, half - start, half, v.ndim - 1),
    )


def join(first, second):
    straight = jnp.concatenate([first, second], axis=-1)
    if not two_way():
        return straight
    crossed = jnp.concatenate([second, first], axis=-1)
    return jnp.where(lax.axis_index("fsdp") == 0, straight, crossed)


def collect(left, right):
    if two_way():
        got = across(dot(left[1], right, 0, 0).astype(BF))
        return dot(left[0], right, 0, 0) + got.astype(F32)
    whole = jnp.concatenate([dot(part, right, 0, 0) for part in left], axis=0)
    return lax.psum_scatter(whole, "fsdp", scatter_dimension=0, tiled=True)


def rms(first, second):
    total = jnp.sum(first * first, -1, keepdims=True) + jnp.sum(second * second, -1, keepdims=True)
    return lax.rsqrt(total / (first.shape[-1] + second.shape[-1]) + EPS)


def norm_back(grads, normed, gains, scale):
    m = [g * d for g, d in zip(gains, grads)]
    mean = (
        jnp.sum(m[0] * normed[0], -1, keepdims=True) + jnp.sum(m[1] * normed[1], -1, keepdims=True)
    ) / (m[0].shape[-1] + m[1].shape[-1])
    return [scale * (a - n * mean) for a, n in zip(m, normed)]


def local(
    tokens,
    attn_qkv,
    attn_out,
    norm_gains,
    expert_in,
    expert_out,
    segment_ids,
    keep_mask,
    routes,
    gate_weights,
    cotangent,
):
    tok_count, width = tokens.shape
    head_width = attn_qkv.shape[2]
    seq_count = tok_count // SEQ_LEN
    own_experts, hidden_width = expert_in.shape[2:]
    columns = own_experts * hidden_width
    rank = lax.axis_index("heads") * lax.axis_size("tensor") + lax.axis_index("tensor")
    shard = tok_count // (lax.axis_size("heads") * lax.axis_size("tensor"))

    gains = [g.astype(F32) for g in spread(norm_gains.astype(BF), 1)]
    gain_one, gain_two = [g[0] for g in gains], [g[1] for g in gains]
    w_qkv = spread(attn_qkv.astype(BF).reshape(-1, 3 * head_width))
    w_o = spread(after(attn_out, w_qkv[1]).astype(BF).T, 1)
    w_out = spread(after(expert_out, w_o[1]).astype(BF).reshape(-1, columns))
    w_in = spread(after(expert_in, w_out[1]).astype(BF).reshape(-1, 2 * columns))
    w_o_full = gather_pair(w_o)

    x = halves(tokens.astype(F32))
    r_one = rms(*x)
    h_one = [(v * r_one * g).astype(BF) for v, g in zip(x, gain_one)]
    projected = (dot(h_one[0], w_qkv[0]) + dot(h_one[1], w_qkv[1])).astype(BF)
    q, k, v = [
        projected[:, i * head_width : (i + 1) * head_width].reshape(seq_count, SEQ_LEN, head_width)
        for i in range(3)
    ]
    seg = segment_ids.reshape(seq_count, SEQ_LEN)
    keep = keep_mask.reshape(seq_count, SEQ_LEN)
    diagonal = jnp.arange(SEQ_LEN)[:, None] == jnp.arange(SEQ_LEN)[None, :]
    allowed = (seg[:, :, None] == seg[:, None, :]) & ((keep[:, None, :] == 1) | diagonal[None])
    score_scale = head_width ** (-0.5)
    scores = jnp.einsum("sqe,ske->sqk", q, k, preferred_element_type=F32) * score_scale
    probs = jax.nn.softmax(jnp.where(allowed, scores, -1e30), axis=-1)
    attended = jnp.einsum("sqk,ske->sqe", probs.astype(BF), v, preferred_element_type=F32)
    attended = attended.reshape(tok_count, head_width).astype(BF)

    attended_rows = lax.all_to_all(attended, GROUP, 0, 1, tiled=True)
    x_rows = halves(lax.dynamic_slice_in_dim(tokens, rank * shard, shard, 0).astype(F32))
    middle = [v + dot(attended_rows, w) for v, w in zip(x_rows, w_o_full)]
    r_two = rms(*middle)
    n_two = [v * r_two for v in middle]
    h_two = gather_pair([(n * g).astype(BF) for n, g in zip(n_two, gain_two)])

    first_expert = lax.axis_index("heads") * own_experts
    weights = jnp.concatenate(
        [
            jnp.broadcast_to(
                jnp.sum(
                    jnp.where(routes == first_expert + e, gate_weights, 0.0), 1, keepdims=True
                ),
                (tok_count, hidden_width),
            )
            for e in range(own_experts)
        ],
        axis=1,
    )
    grad_out = halves(cotangent)
    grad_act = weights * (dot(grad_out[0], w_out[0]) + dot(grad_out[1], w_out[1]))
    gate_up = dot(h_two[0], w_in[0]) + dot(h_two[1], w_in[1])
    gate, up = gate_up[:, :columns], gate_up[:, columns:]
    sig = jax.nn.sigmoid(gate)
    silu = gate * sig
    act = (weights * (silu * up)).astype(BF)
    grad_gate_up = jnp.concatenate(
        [grad_act * up * sig * (1.0 + gate * (1.0 - sig)), grad_act * silu], axis=1
    ).astype(BF)
    grad_two = reduce_pair([dot(grad_gate_up, w, 1, 1) for w in w_in])
    grad_two = [g.astype(F32) for g in grad_two]
    expert_out_grad = collect(grad_out, act)
    expert_in_grad = collect(h_two, grad_gate_up)

    mixture = reduce_pair([dot(act, w, 1, 1) for w in w_out])
    out_rows = join(*[(a + b.astype(F32)).astype(BF) for a, b in zip(middle, mixture)])
    half = width // 2
    output = jnp.concatenate(gather_pair([out_rows[:, :half], out_rows[:, half:]]), axis=1)

    out_in_rows = halves(lax.dynamic_slice_in_dim(cotangent, rank * shard, shard, 0).astype(F32))
    grad_middle = [
        a + b for a, b in zip(out_in_rows, norm_back(grad_two, n_two, gain_two, r_two))
    ]
    gain_two_part = join(*[jnp.sum(g * n, axis=0) for g, n in zip(grad_two, n_two)])
    grad_branch_rows = [g.astype(BF) for g in grad_middle]
    grad_attended = (
        dot(grad_branch_rows[0], w_o_full[0], 1, 1) + dot(grad_branch_rows[1], w_o_full[1], 1, 1)
    ).astype(BF)
    grad_attended = lax.all_to_all(grad_attended, GROUP, 1, 0, tiled=True)
    grad_attended = grad_attended.reshape(seq_count, SEQ_LEN, head_width)
    grad_branch = gather_pair(grad_branch_rows)
    out_grad = collect(grad_branch, attended)

    grad_v = jnp.einsum("sqk,sqe->ske", probs.astype(BF), grad_attended, preferred_element_type=F32)
    grad_probs = jnp.einsum("sqe,ske->sqk", grad_attended, v, preferred_element_type=F32)
    grad_scores = probs * (grad_probs - jnp.sum(probs * grad_probs, axis=-1, keepdims=True))
    grad_scores = grad_scores.astype(BF)
    grad_q = jnp.einsum("sqk,ske->sqe", grad_scores, k, preferred_element_type=F32) * score_scale
    grad_k = jnp.einsum("sqk,sqe->ske", grad_scores, q, preferred_element_type=F32) * score_scale
    grad_projected = jnp.concatenate([grad_q, grad_k, grad_v], axis=-1)
    grad_projected = grad_projected.reshape(tok_count, 3 * head_width).astype(BF)
    grad_one_part = [dot(grad_projected, w, 1, 1) for w in w_qkv]
    qkv_grad = collect(h_one, grad_projected)

    gain_one_part = join(
        *[jnp.sum(g * (v * r_one), axis=0) for g, v in zip(grad_one_part, x)]
    )
    gain_parts = lax.psum(jnp.stack([gain_one_part, gain_two_part]), EVERY)
    own_width = norm_gains.shape[1]
    gains_grad = lax.dynamic_slice_in_dim(
        gain_parts, lax.axis_index("fsdp") * own_width, own_width, 1
    )

    grad_one = [g.astype(F32) for g in reduce_pair(grad_one_part)]
    r_rows = rms(*x_rows)
    n_rows = [v * r_rows for v in x_rows]
    grad_rows = join(
        *[a + b for a, b in zip(grad_middle, norm_back(grad_one, n_rows, gain_one, r_rows))]
    ).astype(BF)
    input_grad = jnp.concatenate(
        gather_pair([grad_rows[:, :half], grad_rows[:, half:]]), axis=1
    ).astype(F32)

    return (
        output,
        input_grad,
        qkv_grad.reshape(attn_qkv.shape),
        out_grad,
        gains_grad,
        expert_in_grad.reshape(expert_in.shape),
        expert_out_grad.reshape(expert_out.shape),
    )


def solution(mesh):
    placed = (
        P("fsdp", None),
        P("fsdp", None, ("heads", "tensor")),
        P("fsdp", ("heads", "tensor")),
        P(None, "fsdp"),
        P("fsdp", None, "heads", "tensor"),
        P("fsdp", "heads", "tensor"),
        P("fsdp"),
        P("fsdp"),
        P("fsdp", None),
        P("fsdp", None),
        P("fsdp", None),
    )
    return jax.shard_map(
        local,
        mesh=mesh,
        in_specs=placed,
        out_specs=(
            P("fsdp", None),
            P("fsdp", None),
            P("fsdp", None, ("heads", "tensor")),
            P("fsdp", ("heads", "tensor")),
            P(None, "fsdp"),
            P("fsdp", None, "heads", "tensor"),
            P("fsdp", "heads", "tensor"),
        ),
        check_vma=False,
    )
```

```python
import itertools

import jax
import jax.numpy as jnp
from jax import lax
from jax.experimental import pallas as pl
from jax.experimental.pallas import tpu as pltpu
from jax.sharding import PartitionSpec as P

SEQ_LEN = 1024
EPS = 1e-06
BF = jnp.bfloat16
F32 = jnp.float32
GROUP = ("heads", "tensor")
EVERY = ("fsdp", "heads", "tensor")

STEPS = {
    "core": ("tensor", 1, 0),
    "x": ("tensor", 2, 1),
    "z0": ("heads", 1, 2),
    "z1": ("heads", 2, 3),
}
BITS = (1, 2, 4, 8)
ORDER_A = ("core", "x", "z0", "z1")
ORDER_B = ("core", "z0", "z1", "x")


def dot(a, b, ca=1, cb=0):
    return lax.dot_general(a, b, (((ca,), (cb,)), ((), ())), preferred_element_type=F32)


def after(value, *others):
    return lax.optimization_barrier((value,) + others)[0]


def swap(v, step):
    name, bit, _ = STEPS[step]
    return lax.ppermute(v, name, [(i, i ^ bit) for i in range(lax.axis_size(name))])


def hold(values, *gates):
    return list(lax.optimization_barrier((*values, *gates))[: len(values)])


def reduce_rest(parts, gates=((), (), ()), orders=(ORDER_A, ORDER_B)):
    rows, cols = parts[0].shape
    now = [v.reshape(1, 2, 2, 2, rows // 8, cols) for v in parts]
    sent, after_step = [], []
    for i in range(3):
        now = hold(now, *gates[i])
        steps = [order[i + 1] for order in orders]
        send = [lax.slice_in_dim(v, 1, 2, axis=STEPS[s][2]) for v, s in zip(now, steps)]
        mine = [lax.slice_in_dim(v, 0, 1, axis=STEPS[s][2]) for v, s in zip(now, steps)]
        got = [swap(v, s) for v, s in zip(send, steps)]
        now = [(m.astype(F32) + g.astype(F32)).astype(BF) for m, g in zip(mine, got)]
        sent.append(send)
        after_step.append(now)
    return [v.reshape(rows // 8, cols) for v in now], sent, after_step


def reduce_first(left, rights, *gates):
    half = left.shape[0] // 2
    pair = []
    later = after(left, *gates) if gates else left
    for right in rights:
        got = swap(dot(left[half:], right, 1, 1).astype(BF), "core")
        pair.append((dot(later[:half], right, 1, 1) + got.astype(F32)).astype(BF))
    return pair


def gather_chain(parts, gates=((), (), (), ()), orders=(ORDER_A, ORDER_B), vector=None):
    rows, cols = parts[0].shape
    now = [v.reshape(1, 1, 1, 1, rows, cols) for v in parts]
    stages = []
    for i in range(4):
        now = hold(now, *gates[i], *([] if vector is None else [vector]))
        if vector is not None:
            vector = vector + swap(vector, ORDER_A[i])
        steps = [order[3 - i] for order in orders]
        got = [swap(v, step) for v, step in zip(now, steps)]
        if i < 3:
            now = [
                jnp.concatenate([v, g], axis=STEPS[step][2])
                for v, g, step in zip(now, got, steps)
            ]
            stages.append(now)
    flat_rows = [[v.reshape(8 * rows, cols) for v in pair] for pair in zip(now, got)]
    return flat_rows, stages, vector


def whole(pairs):
    return [jnp.concatenate(pair, axis=0) for pair in pairs]


def reversed_bits(p):
    return sum(((p >> i) & 1) << (3 - i) for i in range(4))


def group_index():
    return lax.axis_index("heads") * lax.axis_size("tensor") + lax.axis_index("tensor")


def reversed_index():
    me = group_index()
    return sum(((me >> i) & 1) << (3 - i) for i in range(4))


def reorder(parts, start, dtype, tile=256, shift=None):
    rows, cols = parts[0].shape
    tile = min(tile, cols)
    per = cols // tile
    count = len(parts)
    block = rows // 16

    def kernel(at, *refs):
        out = refs[-1]
        j = pl.program_id(0)
        for i, part in enumerate(refs[:-1]):

            @pl.when(j // per == i)
            def _(part=part):
                for p in range(16):
                    src = pl.multiple_of((at[0] ^ reversed_bits(p)) * block, block)
                    out[p * block : (p + 1) * block, :] = part[pl.ds(src, block), :].astype(dtype)

    def spec(i):
        def where(j, at):
            k = jnp.clip(j - i * per, 0, per - 1)
            return (0, lax.rem(k + at[1], per))

        return pl.BlockSpec((rows, tile), where)

    at = jnp.stack([start, jnp.int32(0) if shift is None else shift // tile]).astype(jnp.int32)
    return pl.pallas_call(
        kernel,
        grid_spec=pltpu.PrefetchScalarGridSpec(
            num_scalar_prefetch=1,
            grid=(per * count,),
            in_specs=[spec(i) for i in range(count)],
            out_specs=pl.BlockSpec((rows, tile), lambda j, at: (0, j)),
        ),
        out_shape=jax.ShapeDtypeStruct((rows, cols * count), dtype),
        cost_estimate=pl.CostEstimate(
            flops=0, bytes_accessed=rows * cols * count * 8, transcendentals=0
        ),
    )(at, *parts)


VMEM_LIMIT = 48 * 2**20


def indices(shape, order):
    lead = shape[1:-1]
    spots = itertools.product(*[range(lead[i]) for i in order])
    return [tuple(spot[order.index(i)] for i in range(len(lead))) for spot in spots]


def flat(weights, orders):
    rows = min(256, weights[0].shape[0])
    spots = [indices(v.shape, order) for v, order in zip(weights, orders)]
    wide = weights[0].shape[-1]
    columns = sum(len(s) for s in spots) * wide

    def kernel(*refs):
        out, at = refs[-1], 0
        for ref, some in zip(refs, spots):
            for spot in some:
                out[:, at : at + wide] = ref[(slice(None), *spot, slice(None))].astype(BF)
                at += wide

    def spec(v):
        zeros = (0,) * (v.ndim - 1)
        return pl.BlockSpec((rows, *v.shape[1:]), lambda i: (i, *zeros))

    count = weights[0].shape[0]
    return pl.pallas_call(
        kernel,
        grid=(count // rows,),
        in_specs=[spec(v) for v in weights],
        out_specs=pl.BlockSpec((rows, columns), lambda i: (i, 0)),
        out_shape=jax.ShapeDtypeStruct((count, columns), BF),
        compiler_params=pltpu.CompilerParams(vmem_limit_bytes=VMEM_LIMIT),
        cost_estimate=pl.CostEstimate(
            flops=0, bytes_accessed=count * columns * 6, transcendentals=0
        ),
    )(*weights)


def unflat_sum(own, got, shape, order):
    rows, wide = min(256, shape[0]), shape[-1]
    spots = indices(shape, order)

    def kernel(own_ref, got_ref, out):
        for j, spot in enumerate(spots):
            here = slice(j * wide, (j + 1) * wide)
            out[(slice(None), *spot, slice(None))] = own_ref[:, here] + got_ref[:, here].astype(F32)

    zeros = (0,) * (len(shape) - 1)
    return pl.pallas_call(
        kernel,
        grid=(shape[0] // rows,),
        in_specs=[
            pl.BlockSpec((rows, own.shape[1]), lambda i: (i, 0)),
            pl.BlockSpec((rows, own.shape[1]), lambda i: (i, 0)),
        ],
        out_specs=pl.BlockSpec((rows, *shape[1:]), lambda i: (i, *zeros)),
        out_shape=jax.ShapeDtypeStruct(shape, F32),
        compiler_params=pltpu.CompilerParams(vmem_limit_bytes=VMEM_LIMIT),
        cost_estimate=pl.CostEstimate(flops=0, bytes_accessed=own.size * 10, transcendentals=0),
    )(own, got)


def experts(first, named, top, h, grad_out, weights, count):
    tokens, half = h[0].shape
    wide = weights[0].shape[1] // (3 * count)
    rows = min(1024, tokens)

    def kernel(first_ref, named_ref, ha, hb, wa, wb, ga, gb, oa, ob, act_ref, grad_ref):
        mine = (first_ref[0] + pl.program_id(0)).astype(F32)
        named = named_ref[...]
        weight = jnp.sum(
            jnp.where(named[:, :top] == mine, named[:, top : 2 * top], 0.0), 1, keepdims=True
        )
        grad = weight * (dot(ga[...], oa[...]) + dot(gb[...], ob[...]))
        both = dot(ha[...], wa[...]) + dot(hb[...], wb[...])
        gate, up = both[:, :wide], both[:, wide:]
        sig = 1.0 / (1.0 + jnp.exp(-gate))
        silu = gate * sig
        act_ref[...] = (weight * (silu * up)).astype(BF)
        grad_ref[:, :wide] = (grad * up * sig * (1.0 + gate * (1.0 - sig))).astype(BF)
        grad_ref[:, wide:] = (grad * silu).astype(BF)

    def by_rows(columns):
        return pl.BlockSpec((rows, columns), lambda e, r: (r, 0))

    def by_expert(columns, skip):
        return pl.BlockSpec((half, columns), lambda e, r: (0, skip + e))

    def out(columns):
        return pl.BlockSpec((rows, columns), lambda e, r: (r, e))

    return pl.pallas_call(
        kernel,
        grid=(count, tokens // rows),
        in_specs=[
            pl.BlockSpec(memory_space=pltpu.SMEM),
            by_rows(128),
            by_rows(half),
            by_rows(half),
            by_expert(2 * wide, 0),
            by_expert(2 * wide, 0),
            by_rows(half),
            by_rows(half),
            by_expert(wide, 2 * count),
            by_expert(wide, 2 * count),
        ],
        out_specs=[out(wide), out(2 * wide)],
        out_shape=[
            jax.ShapeDtypeStruct((tokens, count * wide), BF),
            jax.ShapeDtypeStruct((tokens, 2 * count * wide), BF),
        ],
        compiler_params=pltpu.CompilerParams(vmem_limit_bytes=VMEM_LIMIT),
        cost_estimate=pl.CostEstimate(
            flops=12 * tokens * half * count * wide,
            bytes_accessed=16 * tokens * half + 12 * half * count * wide,
            transcendentals=tokens * count * wide,
        ),
    )(first.reshape(1), named, *h, *weights, *grad_out, *weights)


def ordered(pairs, start, dtype, tile=512):
    rows, cols = pairs[0][0].shape
    per, block = cols // tile, rows // 8

    def kernel(at, *refs):
        out, j = refs[-1], pl.program_id(0)
        for i in range(len(pairs)):
            for top in range(2):

                @pl.when((j // per == i) & (at[0] // 8 == top))
                def _(i=i, top=top):
                    for p in range(16):
                        part = refs[2 * i + (top ^ (p & 1))]
                        src = pl.multiple_of(((at[0] ^ reversed_bits(p)) & 7) * block, block)
                        out[p * block : (p + 1) * block, :] = part[pl.ds(src, block), :].astype(
                            dtype
                        )

    def spec(i):
        return pl.BlockSpec((rows, tile), lambda j, at: (0, jnp.clip(j - i * per, 0, per - 1)))

    return pl.pallas_call(
        kernel,
        grid_spec=pltpu.PrefetchScalarGridSpec(
            num_scalar_prefetch=1,
            grid=(per * len(pairs),),
            in_specs=[spec(i) for i in range(len(pairs)) for _ in range(2)],
            out_specs=pl.BlockSpec((2 * rows, tile), lambda j, at: (0, j)),
        ),
        out_shape=jax.ShapeDtypeStruct((2 * rows, cols * len(pairs)), dtype),
        compiler_params=pltpu.CompilerParams(vmem_limit_bytes=VMEM_LIMIT),
        cost_estimate=pl.CostEstimate(
            flops=0, bytes_accessed=rows * cols * len(pairs) * 12, transcendentals=0
        ),
    )(start.reshape(1).astype(jnp.int32), *[v for pair in pairs for v in pair])


def two_way():
    return lax.axis_size("fsdp") == 2


def across(v):
    return v if v is None else lax.ppermute(v, "fsdp", [(0, 1), (1, 0)])


def spread(v, axis=0):
    if two_way():
        return v, across(v)
    full = lax.all_gather(v, "fsdp", axis=axis, tiled=True)
    half = full.shape[axis] // 2
    return (
        lax.slice_in_dim(full, 0, half, axis=axis),
        lax.slice_in_dim(full, half, 2 * half, axis=axis),
    )


def halves(v):
    half = v.shape[-1] // 2
    start = lax.axis_index("fsdp") * half if two_way() else 0
    return (
        lax.dynamic_slice_in_dim(v, start, half, v.ndim - 1),
        lax.dynamic_slice_in_dim(v, half - start, half, v.ndim - 1),
    )


def join(first, second):
    straight = jnp.concatenate([first, second], axis=-1)
    if not two_way():
        return straight
    crossed = jnp.concatenate([second, first], axis=-1)
    return jnp.where(lax.axis_index("fsdp") == 0, straight, crossed)


def partner_part(left, right):
    return dot(left[1], right, 0, 0).astype(BF) if two_way() else None


def own_part(left, right):
    if two_way():
        return dot(left[0], right, 0, 0)
    whole = jnp.concatenate([dot(part, right, 0, 0) for part in left], axis=0)
    return lax.psum_scatter(whole, "fsdp", scatter_dimension=0, tiled=True)


def beside(*parts):
    return jnp.concatenate(parts, axis=1) if two_way() else None


def restore(own, got, shape, order):
    if two_way():
        return unflat_sum(own, got, shape, order)
    lead = [shape[1 + i] for i in order]
    turned = own.reshape(shape[0], *lead, shape[-1])
    back = [1 + order.index(i) for i in range(len(order))]
    return turned.transpose(0, *back, len(shape) - 1)


def rms(first, second):
    total = jnp.sum(first * first, -1, keepdims=True) + jnp.sum(second * second, -1, keepdims=True)
    return lax.rsqrt(total / (first.shape[-1] + second.shape[-1]) + EPS)


def norm_back(grads, normed, gains, scale):
    m = [g * d for g, d in zip(gains, grads)]
    mean = (
        jnp.sum(m[0] * normed[0], -1, keepdims=True) + jnp.sum(m[1] * normed[1], -1, keepdims=True)
    ) / (m[0].shape[-1] + m[1].shape[-1])
    return [scale * (a - n * mean) for a, n in zip(m, normed)]


def local(
    tokens,
    attn_qkv,
    attn_out,
    norm_gains,
    expert_in,
    expert_out,
    segment_ids,
    keep_mask,
    routes,
    gate_weights,
    cotangent,
):
    tok_count, width = tokens.shape
    head_width = attn_qkv.shape[2]
    seq_count = tok_count // SEQ_LEN
    own_experts, hidden_width = expert_in.shape[2:]
    columns = own_experts * hidden_width
    rank, rank_reversed = group_index(), reversed_index()
    shard = tok_count // 16
    half = width // 2

    gains = [g.astype(F32) for g in spread(norm_gains.astype(BF), 1)]
    gain_one, gain_two = [g[0] for g in gains], [g[1] for g in gains]
    w_qkv = spread(attn_qkv.astype(BF).reshape(-1, 3 * head_width))
    w_o_own = after(attn_out.astype(BF).T, w_qkv[0])
    w_o = spread(w_o_own, 1)
    w_experts = flat([expert_in, expert_out], [(1, 0), (0,)])
    w_qkv = w_qkv[0], after(w_qkv[1], w_experts)
    w_experts = spread(after(w_experts, w_qkv[1]))
    w_in = [w[:, : 2 * columns] for w in w_experts]
    w_out = [w[:, 2 * columns :] for w in w_experts]

    x = [v.astype(F32) for v in halves(tokens)]
    r_one = rms(*x)
    h_one = [(v * r_one * g).astype(BF) for v, g in zip(x, gain_one)]
    projected = (dot(h_one[0], w_qkv[0]) + dot(h_one[1], w_qkv[1])).astype(BF)
    w_o = w_o[0], after(w_o[1], projected)
    w_o_full = [lax.all_gather(w, GROUP, axis=0, tiled=True) for w in w_o]
    q, k, v = [
        projected[:, i * head_width : (i + 1) * head_width].reshape(seq_count, SEQ_LEN, head_width)
        for i in range(3)
    ]
    seg = segment_ids.reshape(seq_count, SEQ_LEN)
    keep = keep_mask.reshape(seq_count, SEQ_LEN)
    diagonal = jnp.arange(SEQ_LEN)[:, None] == jnp.arange(SEQ_LEN)[None, :]
    allowed = (seg[:, :, None] == seg[:, None, :]) & ((keep[:, None, :] == 1) | diagonal[None])
    score_scale = head_width ** (-0.5)
    scores = jnp.einsum("sqe,ske->sqk", q, k, preferred_element_type=F32) * score_scale
    probs = jax.nn.softmax(jnp.where(allowed, scores, -1e30), axis=-1)
    attended = jnp.einsum("sqk,ske->sqe", probs.astype(BF), v, preferred_element_type=F32)
    attended = attended.reshape(tok_count, head_width).astype(BF)

    attended_rows = lax.all_to_all(attended, GROUP, 0, 1, tiled=True)
    first_expert = lax.axis_index("heads") * own_experts
    named = jnp.concatenate([routes.astype(F32), gate_weights], axis=1)
    top = routes.shape[1]
    named = jnp.pad(named, ((0, 0), (0, 128 - 2 * top)))
    named = reorder([named], rank, F32)
    attended_rows = after(attended_rows, named)
    start = lax.axis_index("fsdp") * half if two_way() else jnp.int32(0)
    grad_out = reorder([cotangent], rank, BF, shift=start)
    attended_rows = after(attended_rows, grad_out)
    grad_out = grad_out[:, :half], grad_out[:, half:]
    x_rows = halves(lax.dynamic_slice_in_dim(tokens, rank * shard, shard, 0))
    x_rows = [v.astype(F32) for v in x_rows]
    middle = [v + dot(attended_rows, w) for v, w in zip(x_rows, w_o_full)]
    r_two = rms(*middle)
    n_two = [v * r_two for v in middle]
    h_two_rows = [(n * g).astype(BF) for n, g in zip(n_two, gain_two)]
    h_two = whole(gather_chain(h_two_rows)[0])

    act, grad_gate_up = experts(first_expert, named, top, h_two, grad_out, w_experts, own_experts)
    grad_two = reduce_first(grad_gate_up, w_in)
    act_late, grad_gate_up_late = hold([act, grad_gate_up], *grad_two)
    expert_in_part = partner_part(h_two, grad_gate_up_late)
    expert_in_got = across(expert_in_part)
    expert_out_part = partner_part(grad_out, after(act_late, expert_in_part))
    expert_out_got = across(expert_out_part)
    grad_two, _, steps_two = reduce_rest(
        grad_two, ((), [expert_in_part], [expert_out_part])
    )
    grad_two = [g.astype(F32) for g in grad_two]

    out_in_rows = halves(lax.dynamic_slice_in_dim(cotangent, rank * shard, shard, 0))
    out_in_rows = [v.astype(F32) for v in out_in_rows]
    grad_middle = [
        a + b for a, b in zip(out_in_rows, norm_back(grad_two, n_two, gain_two, r_two))
    ]
    gain_two_part = join(*[jnp.sum(g * n, axis=0) for g, n in zip(grad_two, n_two)])
    grad_branch_rows = [g.astype(BF) for g in grad_middle]
    grad_attended_rows = (
        dot(grad_branch_rows[0], w_o_full[0], 1, 1) + dot(grad_branch_rows[1], w_o_full[1], 1, 1)
    ).astype(BF)
    grad_attended = lax.all_to_all(grad_attended_rows, GROUP, 1, 0, tiled=True)
    grad_attended = grad_attended.reshape(seq_count, SEQ_LEN, head_width)

    grad_v = jnp.einsum("sqk,sqe->ske", probs.astype(BF), grad_attended, preferred_element_type=F32)
    grad_probs = jnp.einsum("sqe,ske->sqk", grad_attended, v, preferred_element_type=F32)
    grad_scores = probs * (grad_probs - jnp.sum(probs * grad_probs, axis=-1, keepdims=True))
    grad_scores = grad_scores.astype(BF)
    grad_q = jnp.einsum("sqk,ske->sqe", grad_scores, k, preferred_element_type=F32) * score_scale
    grad_k = jnp.einsum("sqk,sqe->ske", grad_scores, q, preferred_element_type=F32) * score_scale
    grad_projected = jnp.concatenate([grad_q, grad_k, grad_v], axis=-1)
    grad_projected = grad_projected.reshape(tok_count, 3 * head_width).astype(BF)
    grad_projected_blocks = reorder([grad_projected], rank, BF, tile=3 * head_width)
    grad_one = reduce_first(grad_projected_blocks, w_qkv)
    qkv_part = partner_part(h_one, after(grad_projected, *grad_one))

    mixture = reduce_first(after(act_late, *steps_two[1]), w_out, grad_attended_rows)
    mixture = reduce_rest(mixture, ((), [grad_projected_blocks], grad_one))[0]
    grad_branch = jnp.concatenate(hold(grad_branch_rows, grad_attended_rows), axis=1)
    grad_branch = lax.all_gather(grad_branch, GROUP, axis=0, tiled=True)
    out_rows = join(*[(a + b.astype(F32)).astype(BF) for a, b in zip(middle, mixture)])
    output = lax.all_gather(after(out_rows, grad_branch), GROUP, axis=0, tiled=True)
    grad_branch = grad_branch[:, :half], grad_branch[:, half:]
    out_part = partner_part(grad_branch, attended)
    attention_got = across(beside(qkv_part, out_part))
    grad_one, _, steps_one = reduce_rest(grad_one, ((), [qkv_part], [mixture[0], expert_in_got]))
    own_act, own_gate_up = hold([act, grad_gate_up], grad_attended_rows)
    expert_in_own = own_part(h_two, own_gate_up)
    expert_out_own = own_part(grad_out, after(own_act, *steps_one[0]))
    expert_in_grad = restore(
        expert_in_own, after(expert_in_got, *steps_one[1]), expert_in.shape, (1, 0)
    )
    grad_one = hold(grad_one, expert_in_grad, expert_out_own)
    grad_one = [g.astype(F32) for g in grad_one]

    r_rows = rms(*x_rows)
    n_rows = [v * r_rows for v in x_rows]
    gain_one_part = join(*[jnp.sum(g * n, axis=0) for g, n in zip(grad_one, n_rows)])
    gain_parts = jnp.stack([gain_one_part, gain_two_part])
    grad_rows = join(
        *[a + b for a, b in zip(grad_middle, norm_back(grad_one, n_rows, gain_one, r_rows))]
    ).astype(BF)
    expert_out_grad = restore(expert_out_own, expert_out_got, expert_out.shape, (0,))
    input_grad, stages, gain_parts = gather_chain(
        [grad_rows[:, :half], grad_rows[:, half:]],
        ((), (), [expert_out_got], [expert_out_grad, output, attention_got]),
        vector=gain_parts,
    )
    gain_parts = gain_parts + across(gain_parts) if two_way() else lax.psum(gain_parts, "fsdp")
    own_width = norm_gains.shape[1]
    gains_grad = lax.dynamic_slice_in_dim(
        gain_parts, lax.axis_index("fsdp") * own_width, own_width, 1
    )

    qkv_own, out_own = own_part(h_one, grad_projected), own_part(grad_branch, attended)
    if two_way():
        attention_got = attention_got.astype(F32)
        qkv_own = qkv_own + attention_got[:, : 3 * head_width]
        out_own = out_own + attention_got[:, 3 * head_width :]
    input_grad = ordered(input_grad, rank_reversed, F32)

    return (
        output,
        input_grad,
        qkv_own.reshape(attn_qkv.shape),
        out_own,
        gains_grad,
        expert_in_grad,
        expert_out_grad,
    )


def solution(mesh):
    placed = (
        P("fsdp", None),
        P("fsdp", None, ("heads", "tensor")),
        P("fsdp", ("heads", "tensor")),
        P(None, "fsdp"),
        P("fsdp", None, "heads", "tensor"),
        P("fsdp", "heads", "tensor"),
        P("fsdp"),
        P("fsdp"),
        P("fsdp", None),
        P("fsdp", None),
        P("fsdp", None),
    )
    return jax.shard_map(
        local,
        mesh=mesh,
        in_specs=placed,
        out_specs=(
            P("fsdp", None),
            P("fsdp", None),
            P("fsdp", None, ("heads", "tensor")),
            P("fsdp", ("heads", "tensor")),
            P(None, "fsdp"),
            P("fsdp", None, "heads", "tensor"),
            P("fsdp", "heads", "tensor"),
        ),
        check_vma=False,
    )
```

```python
import itertools

import jax
import jax.numpy as jnp
from jax import lax
from jax.experimental import pallas as pl
from jax.experimental.pallas import tpu as pltpu
from jax.sharding import PartitionSpec as P

SEQ_LEN = 1024
EPS = 1e-06
BF = jnp.bfloat16
F32 = jnp.float32
GROUP = ("heads", "tensor")
EVERY = ("fsdp", "heads", "tensor")

STEPS = {
    "core": ("tensor", 1, 0),
    "x": ("tensor", 2, 1),
    "z0": ("heads", 1, 2),
    "z1": ("heads", 2, 3),
}
BITS = (1, 2, 4, 8)
ORDER_A = ("core", "x", "z0", "z1")
ORDER_B = ("core", "z0", "z1", "x")


PLAN = {
    "make": {
        "core2": ("in0", "in0_got"),
        "two1": ("in1", "in1_got", "out", "out_got"),
        "two2": ("mix_send",),
        "do": ("branch", "mix0", "mix1"),
        "blocks": ("mix2",),
        "core1": ("qkv",),
        "one1": ("mix3",),
        "one2": ("in_whole", "attention", "attention_got"),
        "one3": ("output",),
        "stage1": ("out_whole",),
    },
    "wait": {
        "two1": ("in0",),
        "two2": ("out",),
        "one1": ("qkv",),
        "one2": ("in0_got",),
        "one3": ("in_whole", "mix3"),
        "stage1": ("out_got",),
        "stage2": ("output", "out_whole", "attention_got"),
    },
}


def dot(a, b, ca=1, cb=0):
    return lax.dot_general(a, b, (((ca,), (cb,)), ((), ())), preferred_element_type=F32)


def after(value, *others):
    return lax.optimization_barrier((value,) + others)[0]


def swap(v, step):
    name, bit, _ = STEPS[step]
    return lax.ppermute(v, name, [(i, i ^ bit) for i in range(lax.axis_size(name))])


def hold(values, *gates):
    return list(lax.optimization_barrier((*values, *gates))[: len(values)])


def reduce_step(v, step):
    dim = STEPS[step][2]
    got = swap(lax.slice_in_dim(v, 1, 2, axis=dim), step)
    return (lax.slice_in_dim(v, 0, 1, axis=dim).astype(F32) + got.astype(F32)).astype(BF)


def chain_step(parts, i):
    return [reduce_step(v, order[i]) for v, order in zip(parts, (ORDER_A, ORDER_B))]


def reduce_first(left, rights, *gates):
    half = left.shape[0] // 2
    pair, sends = [], []
    later = after(left, *gates) if gates else left
    for right in rights:
        sends.append(dot(left[half:], right, 1, 1).astype(BF))
        got = swap(sends[-1], "core")
        pair.append((dot(later[:half], right, 1, 1) + got.astype(F32)).astype(BF))
    return pair, sends


def gather_chain(parts, orders=(ORDER_A, ORDER_B), vector=None, event=None):
    rows, cols = parts[0].shape
    now = [v.reshape(1, 1, 1, 1, rows, cols) for v in parts]
    for i in range(4):
        if vector is not None:
            now = hold(now, vector)
            vector = vector + swap(vector, ORDER_A[i])
        steps = [order[3 - i] for order in orders]
        got = [swap(v, step) for v, step in zip(now, steps)]
        if i < 3:
            now = [
                jnp.concatenate([v, g], axis=STEPS[step][2])
                for v, g, step in zip(now, got, steps)
            ]
            if event is not None:
                now = event("stage%d" % i, now)
    flat_rows = [[v.reshape(8 * rows, cols) for v in pair] for pair in zip(now, got)]
    return flat_rows, vector


def whole(pairs):
    return [jnp.concatenate(pair, axis=0) for pair in pairs]


def reversed_bits(p):
    return sum(((p >> i) & 1) << (3 - i) for i in range(4))


def group_index():
    return lax.axis_index("heads") * lax.axis_size("tensor") + lax.axis_index("tensor")


def reversed_index():
    me = group_index()
    return sum(((me >> i) & 1) << (3 - i) for i in range(4))


def reorder(parts, start, dtype, tile=256, shift=None):
    rows, cols = parts[0].shape
    tile = min(tile, cols)
    per = cols // tile
    count = len(parts)
    block = rows // 16

    def kernel(at, *refs):
        out = refs[-1]
        j = pl.program_id(0)
        for i, part in enumerate(refs[:-1]):

            @pl.when(j // per == i)
            def _(part=part):
                for p in range(16):
                    src = pl.multiple_of((at[0] ^ reversed_bits(p)) * block, block)
                    out[p * block : (p + 1) * block, :] = part[pl.ds(src, block), :].astype(dtype)

    def spec(i):
        def where(j, at):
            k = jnp.clip(j - i * per, 0, per - 1)
            return (0, lax.rem(k + at[1], per))

        return pl.BlockSpec((rows, tile), where)

    at = jnp.stack([start, jnp.int32(0) if shift is None else shift // tile]).astype(jnp.int32)
    return pl.pallas_call(
        kernel,
        grid_spec=pltpu.PrefetchScalarGridSpec(
            num_scalar_prefetch=1,
            grid=(per * count,),
            in_specs=[spec(i) for i in range(count)],
            out_specs=pl.BlockSpec((rows, tile), lambda j, at: (0, j)),
        ),
        out_shape=jax.ShapeDtypeStruct((rows, cols * count), dtype),
        cost_estimate=pl.CostEstimate(
            flops=0, bytes_accessed=rows * cols * count * 8, transcendentals=0
        ),
    )(at, *parts)


VMEM_LIMIT = 48 * 2**20


def indices(shape, order):
    lead = shape[1:-1]
    spots = itertools.product(*[range(lead[i]) for i in order])
    return [tuple(spot[order.index(i)] for i in range(len(lead))) for spot in spots]


def flat(weights, orders):
    rows = min(256, weights[0].shape[0])
    spots = [indices(v.shape, order) for v, order in zip(weights, orders)]
    wide = weights[0].shape[-1]
    columns = sum(len(s) for s in spots) * wide

    def kernel(*refs):
        out, at = refs[-1], 0
        for ref, some in zip(refs, spots):
            for spot in some:
                out[:, at : at + wide] = ref[(slice(None), *spot, slice(None))].astype(BF)
                at += wide

    def spec(v):
        zeros = (0,) * (v.ndim - 1)
        return pl.BlockSpec((rows, *v.shape[1:]), lambda i: (i, *zeros))

    count = weights[0].shape[0]
    return pl.pallas_call(
        kernel,
        grid=(count // rows,),
        in_specs=[spec(v) for v in weights],
        out_specs=pl.BlockSpec((rows, columns), lambda i: (i, 0)),
        out_shape=jax.ShapeDtypeStruct((count, columns), BF),
        compiler_params=pltpu.CompilerParams(vmem_limit_bytes=VMEM_LIMIT),
        cost_estimate=pl.CostEstimate(
            flops=0, bytes_accessed=count * columns * 6, transcendentals=0
        ),
    )(*weights)


def weight_sum(left, right, got, column, shape, order, planes=False):
    rows, wide = min(256, shape[0]), shape[-1]
    tokens, columns = right.shape
    spots = indices(shape, order)
    widths = [columns] if column or len(got) == 1 else [v.shape[1] for v in got]
    homes = [(k, at) for k, w in enumerate(widths) for at in range(0, w, wide)]

    def kernel(left_ref, right_ref, *refs):
        out = refs[-1]
        total = dot(left_ref[...], right_ref[...], 0, 0)
        for j, spot in enumerate(spots):
            k, at = homes[j]
            here = refs[k][:, at : at + wide].astype(F32)
            at = (*spot, slice(None)) if planes else (slice(None), *spot)
            out[(*at, slice(None))] = total[:, j * wide : (j + 1) * wide] + here

    zeros = (0,) * (len(shape) - 1)
    block, where = (rows, *shape[1:]), lambda i: (i, *zeros)
    if planes:
        block, where = (shape[1], rows, wide), lambda i: (0, i, 0)
        shape = (shape[1], shape[0], wide)
    return pl.pallas_call(
        kernel,
        grid=(left.shape[1] // rows,),
        in_specs=[
            pl.BlockSpec((tokens, rows), lambda i: (0, i)),
            pl.BlockSpec((tokens, columns), lambda i: (0, 0)),
        ]
        + [pl.BlockSpec((rows, w), lambda i: (i, column)) for w in widths],
        out_specs=pl.BlockSpec(block, where),
        out_shape=jax.ShapeDtypeStruct(shape, F32),
        compiler_params=pltpu.CompilerParams(vmem_limit_bytes=VMEM_LIMIT),
        cost_estimate=pl.CostEstimate(
            flops=2 * tokens * left.shape[1] * columns,
            bytes_accessed=2 * left.size + 2 * right.size + 6 * left.shape[1] * columns,
            transcendentals=0,
        ),
    )(left, right, *got)


def experts(first, named, top, h, grad_part, grad_rest, weights, count):
    tokens, half = h[0].shape
    wide = weights[0].shape[1] // (3 * count)
    rows = min(1024, tokens)

    def kernel(first_ref, named_ref, ha, hb, wa, wb, part, gb, ob, act_ref, grad_ref):
        mine = (first_ref[0] + pl.program_id(0)).astype(F32)
        named = named_ref[...]
        weight = jnp.sum(
            jnp.where(named[:, :top] == mine, named[:, top : 2 * top], 0.0), 1, keepdims=True
        )
        grad = weight * (part[...] + dot(gb[...], ob[...]))
        both = dot(ha[...], wa[...]) + dot(hb[...], wb[...])
        gate, up = both[:, :wide], both[:, wide:]
        sig = 1.0 / (1.0 + jnp.exp(-gate))
        silu = gate * sig
        act_ref[...] = (weight * (silu * up)).astype(BF)
        grad_ref[:, :wide] = (grad * up * sig * (1.0 + gate * (1.0 - sig))).astype(BF)
        grad_ref[:, wide:] = (grad * silu).astype(BF)

    def by_rows(columns):
        return pl.BlockSpec((rows, columns), lambda e, r: (r, 0))

    def by_expert(columns, skip):
        return pl.BlockSpec((half, columns), lambda e, r: (0, skip + e))

    def out(columns):
        return pl.BlockSpec((rows, columns), lambda e, r: (r, e))

    return pl.pallas_call(
        kernel,
        grid=(count, tokens // rows),
        in_specs=[
            pl.BlockSpec(memory_space=pltpu.SMEM),
            by_rows(128),
            by_rows(half),
            by_rows(half),
            by_expert(2 * wide, 0),
            by_expert(2 * wide, 0),
            out(wide),
            by_rows(half),
            by_expert(wide, 2 * count),
        ],
        out_specs=[out(wide), out(2 * wide)],
        out_shape=[
            jax.ShapeDtypeStruct((tokens, count * wide), BF),
            jax.ShapeDtypeStruct((tokens, 2 * count * wide), BF),
        ],
        compiler_params=pltpu.CompilerParams(vmem_limit_bytes=VMEM_LIMIT),
        cost_estimate=pl.CostEstimate(
            flops=10 * tokens * half * count * wide,
            bytes_accessed=16 * tokens * half + 12 * half * count * wide,
            transcendentals=tokens * count * wide,
        ),
    )(first.reshape(1), named, *h, *weights, grad_part, grad_rest, weights[1])


def ordered(pairs, start, dtype, tile=512):
    rows, cols = pairs[0][0].shape
    per, block = cols // tile, rows // 8

    def kernel(at, *refs):
        out, j = refs[-1], pl.program_id(0)
        for i in range(len(pairs)):
            for top in range(2):

                @pl.when((j // per == i) & (at[0] // 8 == top))
                def _(i=i, top=top):
                    for p in range(16):
                        part = refs[2 * i + (top ^ (p & 1))]
                        src = pl.multiple_of(((at[0] ^ reversed_bits(p)) & 7) * block, block)
                        out[p * block : (p + 1) * block, :] = part[pl.ds(src, block), :].astype(
                            dtype
                        )

    def spec(i):
        return pl.BlockSpec((rows, tile), lambda j, at: (0, jnp.clip(j - i * per, 0, per - 1)))

    return pl.pallas_call(
        kernel,
        grid_spec=pltpu.PrefetchScalarGridSpec(
            num_scalar_prefetch=1,
            grid=(per * len(pairs),),
            in_specs=[spec(i) for i in range(len(pairs)) for _ in range(2)],
            out_specs=pl.BlockSpec((2 * rows, tile), lambda j, at: (0, j)),
        ),
        out_shape=jax.ShapeDtypeStruct((2 * rows, cols * len(pairs)), dtype),
        compiler_params=pltpu.CompilerParams(vmem_limit_bytes=VMEM_LIMIT),
        cost_estimate=pl.CostEstimate(
            flops=0, bytes_accessed=rows * cols * len(pairs) * 12, transcendentals=0
        ),
    )(start.reshape(1).astype(jnp.int32), *[v for pair in pairs for v in pair])


def two_way():
    return lax.axis_size("fsdp") == 2


def across(v):
    return v if v is None else lax.ppermute(v, "fsdp", [(0, 1), (1, 0)])


def spread(v, axis=0):
    if two_way():
        return v, across(v)
    full = lax.all_gather(v, "fsdp", axis=axis, tiled=True)
    half = full.shape[axis] // 2
    return (
        lax.slice_in_dim(full, 0, half, axis=axis),
        lax.slice_in_dim(full, half, 2 * half, axis=axis),
    )


def halves(v):
    half = v.shape[-1] // 2
    start = lax.axis_index("fsdp") * half if two_way() else 0
    return (
        lax.dynamic_slice_in_dim(v, start, half, v.ndim - 1),
        lax.dynamic_slice_in_dim(v, half - start, half, v.ndim - 1),
    )


def join(first, second):
    straight = jnp.concatenate([first, second], axis=-1)
    if not two_way():
        return straight
    crossed = jnp.concatenate([second, first], axis=-1)
    return jnp.where(lax.axis_index("fsdp") == 0, straight, crossed)


def partner_part(left, right):
    return dot(left[1], right, 0, 0).astype(BF)


def beside(*parts):
    return jnp.concatenate(parts, axis=1) if two_way() else None


def weight_grad(left, right, got, column, shape, order, planes=False):
    if two_way():
        total = weight_sum(left[0], right, got, column, shape, order, planes)
        return total.transpose(1, 0, 2) if planes else total
    both = jnp.concatenate([dot(part, right, 0, 0) for part in left], axis=0)
    own = lax.psum_scatter(both, "fsdp", scatter_dimension=0, tiled=True)
    lead = [shape[1 + i] for i in order]
    turned = own.reshape(shape[0], *lead, shape[-1])
    back = [1 + order.index(i) for i in range(len(order))]
    return turned.transpose(0, *back, len(shape) - 1)


def rms(first, second):
    total = jnp.sum(first * first, -1, keepdims=True) + jnp.sum(second * second, -1, keepdims=True)
    return lax.rsqrt(total / (first.shape[-1] + second.shape[-1]) + EPS)


def norm_back(grads, normed, gains, scale):
    m = [g * d for g, d in zip(gains, grads)]
    mean = (
        jnp.sum(m[0] * normed[0], -1, keepdims=True) + jnp.sum(m[1] * normed[1], -1, keepdims=True)
    ) / (m[0].shape[-1] + m[1].shape[-1])
    return [scale * (a - n * mean) for a, n in zip(m, normed)]


def local(
    tokens,
    attn_qkv,
    attn_out,
    norm_gains,
    expert_in,
    expert_out,
    segment_ids,
    keep_mask,
    routes,
    gate_weights,
    cotangent,
):
    tok_count, width = tokens.shape
    head_width = attn_qkv.shape[2]
    seq_count = tok_count // SEQ_LEN
    own_experts, hidden_width = expert_in.shape[2:]
    columns = own_experts * hidden_width
    rank, rank_reversed = group_index(), reversed_index()
    shard = tok_count // 16
    half = width // 2

    gains = [g.astype(F32) for g in spread(norm_gains.astype(BF), 1)]
    gain_one, gain_two = [g[0] for g in gains], [g[1] for g in gains]
    w_qkv = spread(attn_qkv.astype(BF).reshape(-1, 3 * head_width))
    w_o_own = after(attn_out.astype(BF).T, w_qkv[0])
    w_o = spread(w_o_own, 1)
    w_experts_own = flat([expert_in, expert_out], [(1, 0), (0,)])
    w_experts = spread(after(w_experts_own, w_o_own))
    w_in = [w[:, : 2 * columns] for w in w_experts]
    w_out = [w[:, 2 * columns :] for w in w_experts]

    x = [v.astype(F32) for v in halves(after(tokens, w_experts_own))]
    r_one = rms(*x)
    h_one = [(v * r_one * g).astype(BF) for v, g in zip(x, gain_one)]
    projected = (dot(h_one[0], w_qkv[0]) + dot(h_one[1], w_qkv[1])).astype(BF)
    w_o = w_o[0], after(w_o[1], projected)
    w_o_full = [lax.all_gather(w, GROUP, axis=0, tiled=True) for w in w_o]
    q, k, v = [
        projected[:, i * head_width : (i + 1) * head_width].reshape(seq_count, SEQ_LEN, head_width)
        for i in range(3)
    ]
    seg = segment_ids.reshape(seq_count, SEQ_LEN)
    keep = keep_mask.reshape(seq_count, SEQ_LEN)
    diagonal = jnp.arange(SEQ_LEN)[:, None] == jnp.arange(SEQ_LEN)[None, :]
    allowed = (seg[:, :, None] == seg[:, None, :]) & ((keep[:, None, :] == 1) | diagonal[None])
    score_scale = head_width ** (-0.5)
    scores = jnp.einsum("sqe,ske->sqk", q, k, preferred_element_type=F32) * score_scale
    probs = jax.nn.softmax(jnp.where(allowed, scores, -1e30), axis=-1)
    attended = jnp.einsum("sqk,ske->sqe", probs.astype(BF), v, preferred_element_type=F32)
    attended = attended.reshape(tok_count, head_width).astype(BF)

    attended_rows = lax.all_to_all(attended, GROUP, 0, 1, tiled=True)
    first_expert = lax.axis_index("heads") * own_experts
    named = jnp.concatenate([routes.astype(F32), gate_weights], axis=1)
    top = routes.shape[1]
    named = jnp.pad(named, ((0, 0), (0, 128 - 2 * top)))
    named = reorder([named], rank, F32)
    attended_rows = after(attended_rows, named)
    start = lax.axis_index("fsdp") * half if two_way() else jnp.int32(0)
    grad_out = reorder([cotangent], rank, BF, shift=start)
    attended_rows = after(attended_rows, grad_out)
    grad_out = grad_out[:, :half], grad_out[:, half:]
    grad_act_own = dot(grad_out[0], w_out[0])
    attended_rows = after(attended_rows, grad_act_own)
    x_rows = halves(lax.dynamic_slice_in_dim(tokens, rank * shard, shard, 0))
    x_rows = [v.astype(F32) for v in x_rows]
    middle = [v + dot(attended_rows, w) for v, w in zip(x_rows, w_o_full)]
    r_two = rms(*middle)
    n_two = [v * r_two for v in middle]
    h_two_rows = [(n * g).astype(BF) for n, g in zip(n_two, gain_two)]
    h_two = whole(gather_chain(h_two_rows)[0])

    act, grad_gate_up = experts(
        first_expert, named, top, h_two, grad_act_own, grad_out[1], w_experts, own_experts
    )
    done = {}

    def weight_part(left, right, begin, end):
        def make(gates):
            if not two_way() or begin == end:
                return ()
            return partner_part(left, after(right, *gates)[:, begin:end])

        return make

    def moved(name):
        return lambda gates: jax.tree.map(across, done[name])

    def mixture_step(before, i):
        return lambda gates: chain_step(hold(done[before], *gates), i)

    def mixture_sends(gates):
        left = after(act, *gates)[tok_count // 2 :]
        return [dot(left, w, 1, 1).astype(BF) for w in w_out]

    def mixture_core(gates):
        left = after(act, *gates)[: tok_count // 2]
        pair = [
            (dot(left, w, 1, 1) + swap(v, "core").astype(F32)).astype(BF)
            for w, v in zip(w_out, done["mix_send"])
        ]
        return [v.reshape(1, 2, 2, 2, shard, half) for v in pair]

    def gather_branch(gates):
        rows = jnp.concatenate(hold(grad_branch_rows, *gates), axis=1)
        return lax.all_gather(rows, GROUP, axis=0, tiled=True)

    def gather_output(gates):
        pair = [v.reshape(shard, half) for v in done["mix3"]]
        rows = join(*[(a + b.astype(F32)).astype(BF) for a, b in zip(middle, pair)])
        return lax.all_gather(after(rows, done["branch"]), GROUP, axis=0, tiled=True)

    def branch_halves():
        return done["branch"][:, :half], done["branch"][:, half:]

    def attention_parts(gates):
        if not two_way():
            return ()
        return beside(done["qkv"], partner_part(branch_halves(), attended))

    def expert_in_whole(gates):
        moves = jax.tree.leaves((done["in0_got"], done["in1_got"]))
        right = after(grad_gate_up, *gates)
        return weight_grad(h_two, right, moves, 0, expert_in.shape, (1, 0))

    def expert_out_whole(gates):
        right = after(act, *gates)
        return weight_grad(grad_out, right, [done["out_got"]], 0, expert_out.shape, (0,))

    split = 2 * columns
    make = {
        "in0": weight_part(h_two, grad_gate_up, 0, split),
        "in0_got": moved("in0"),
        "in1": weight_part(h_two, grad_gate_up, split, 2 * columns),
        "in1_got": moved("in1"),
        "out": weight_part(grad_out, act, 0, columns),
        "out_got": moved("out"),
        "mix_send": mixture_sends,
        "mix0": mixture_core,
        "mix1": mixture_step("mix0", 1),
        "mix2": mixture_step("mix1", 2),
        "mix3": mixture_step("mix2", 3),
        "branch": gather_branch,
        "output": gather_output,
        "qkv": lambda gates: partner_part(h_one, after(grad_projected, *gates)),
        "attention": attention_parts,
        "attention_got": moved("attention"),
        "in_whole": expert_in_whole,
        "out_whole": expert_out_whole,
    }

    def event(name, values):
        waits = [v for piece in PLAN["wait"].get(name, ()) for v in jax.tree.leaves(done[piece])]
        values = hold(values, *waits)
        for piece in PLAN["make"].get(name, ()):
            done[piece] = make[piece](values)
        return values

    grad_two, _ = reduce_first(grad_gate_up, w_in)
    event("core2", grad_two)
    chain = [v.reshape(1, 2, 2, 2, shard, half) for v in grad_two]
    for i, name in ((1, "two1"), (2, "two2"), (3, "two3")):
        chain = event(name, chain_step(chain, i))
    grad_two = [v.reshape(shard, half).astype(F32) for v in chain]

    out_in_rows = halves(lax.dynamic_slice_in_dim(cotangent, rank * shard, shard, 0))
    out_in_rows = [v.astype(F32) for v in out_in_rows]
    grad_middle = [
        a + b for a, b in zip(out_in_rows, norm_back(grad_two, n_two, gain_two, r_two))
    ]
    gain_two_part = join(*[jnp.sum(g * n, axis=0) for g, n in zip(grad_two, n_two)])
    grad_branch_rows = [g.astype(BF) for g in grad_middle]
    grad_attended_rows = (
        dot(grad_branch_rows[0], w_o_full[0], 1, 1) + dot(grad_branch_rows[1], w_o_full[1], 1, 1)
    ).astype(BF)
    event("do", [grad_attended_rows])
    grad_attended = lax.all_to_all(grad_attended_rows, GROUP, 1, 0, tiled=True)
    grad_attended = event("a2a", [grad_attended])[0]
    grad_attended = grad_attended.reshape(seq_count, SEQ_LEN, head_width)

    grad_v = jnp.einsum("sqk,sqe->ske", probs.astype(BF), grad_attended, preferred_element_type=F32)
    grad_probs = jnp.einsum("sqe,ske->sqk", grad_attended, v, preferred_element_type=F32)
    grad_scores = probs * (grad_probs - jnp.sum(probs * grad_probs, axis=-1, keepdims=True))
    grad_scores = grad_scores.astype(BF)
    grad_q = jnp.einsum("sqk,ske->sqe", grad_scores, k, preferred_element_type=F32) * score_scale
    grad_k = jnp.einsum("sqk,sqe->ske", grad_scores, q, preferred_element_type=F32) * score_scale
    grad_q, grad_k = event("qk", [grad_q, grad_k])
    grad_projected = jnp.concatenate([grad_q, grad_k, grad_v], axis=-1)
    grad_projected = grad_projected.reshape(tok_count, 3 * head_width).astype(BF)
    grad_projected_blocks = reorder([grad_projected], rank, BF, tile=3 * head_width)
    event("blocks", [grad_projected_blocks])
    grad_one, _ = reduce_first(grad_projected_blocks, w_qkv)
    chain = event("core1", grad_one)
    chain = [v.reshape(1, 2, 2, 2, shard, half) for v in chain]
    for i, name in ((1, "one1"), (2, "one2"), (3, "one3")):
        chain = event(name, chain_step(chain, i))
    grad_one = [v.reshape(shard, half).astype(F32) for v in chain]

    r_rows = rms(*x_rows)
    n_rows = [v * r_rows for v in x_rows]
    gain_one_part = join(*[jnp.sum(g * n, axis=0) for g, n in zip(grad_one, n_rows)])
    gain_parts = jnp.stack([gain_one_part, gain_two_part])
    grad_rows = join(
        *[a + b for a, b in zip(grad_middle, norm_back(grad_one, n_rows, gain_one, r_rows))]
    ).astype(BF)
    grad_rows = event("rows", [grad_rows])[0]
    input_grad, gain_parts = gather_chain(
        [grad_rows[:, :half], grad_rows[:, half:]], vector=gain_parts, event=event
    )
    event("end", [gain_parts])

    output, expert_in_grad, expert_out_grad = done["output"], done["in_whole"], done["out_whole"]
    attention_got = [done["attention_got"]]
    qkv_grad = weight_grad(h_one, grad_projected, attention_got, 0, attn_qkv.shape, (0,), True)
    out_grad = weight_grad(branch_halves(), attended, attention_got, 3, attn_out.shape, ())
    input_grad = ordered(input_grad, rank_reversed, F32)
    if two_way():
        got = after(across(gain_parts), input_grad, qkv_grad, out_grad, expert_out_grad)
        gain_parts = gain_parts + got
    else:
        gain_parts = lax.psum(gain_parts, "fsdp")
    own_width = norm_gains.shape[1]
    gains_grad = lax.dynamic_slice_in_dim(
        gain_parts, lax.axis_index("fsdp") * own_width, own_width, 1
    )

    return (
        output,
        input_grad,
        qkv_grad,
        out_grad,
        gains_grad,
        expert_in_grad,
        expert_out_grad,
    )


def solution(mesh):
    placed = (
        P("fsdp", None),
        P("fsdp", None, ("heads", "tensor")),
        P("fsdp", ("heads", "tensor")),
        P(None, "fsdp"),
        P("fsdp", None, "heads", "tensor"),
        P("fsdp", "heads", "tensor"),
        P("fsdp"),
        P("fsdp"),
        P("fsdp", None),
        P("fsdp", None),
        P("fsdp", None),
    )
    return jax.shard_map(
        local,
        mesh=mesh,
        in_specs=placed,
        out_specs=(
            P("fsdp", None),
            P("fsdp", None),
            P("fsdp", None, ("heads", "tensor")),
            P("fsdp", ("heads", "tensor")),
            P(None, "fsdp"),
            P("fsdp", None, "heads", "tensor"),
            P("fsdp", "heads", "tensor"),
        ),
        check_vma=False,
    )
```

```python
import itertools

import jax
import jax.numpy as jnp
from jax import lax
from jax.experimental import pallas as pl
from jax.experimental.pallas import tpu as pltpu
from jax.sharding import PartitionSpec as P

SEQ_LEN = 1024
EPS = 1e-06
BF = jnp.bfloat16
F32 = jnp.float32
GROUP = ("heads", "tensor")
EVERY = ("fsdp", "heads", "tensor")

STEPS = {
    "core": ("tensor", 1, 0),
    "x": ("tensor", 2, 1),
    "z0": ("heads", 1, 2),
    "z1": ("heads", 2, 3),
}
BITS = (1, 2, 4, 8)
ORDER_A = ("core", "x", "z0", "z1")
ORDER_B = ("core", "z0", "z1", "x")


PLAN = {
    "make": {
        "core2": ("in0", "in0_got"),
        "two1": ("in1", "in1_got", "out", "out_got"),
        "two2": ("mix_send",),
        "do": ("branch", "mix0", "mix1"),
        "blocks": ("mix2",),
        "core1": ("qkv",),
        "one2": ("mix3", "in_whole", "attention", "attention_got"),
        "one3": ("output",),
        "stage1": ("out_whole",),
    },
    "wait": {
        "two1": ("in0",),
        "two2": ("out",),
        "one1": ("qkv",),
        "one2": ("in0_got",),
        "one3": ("in_whole", "mix3"),
        "stage1": ("out_got",),
        "stage2": ("output", "out_whole", "attention_got"),
    },
}


def dot(a, b, ca=1, cb=0):
    return lax.dot_general(a, b, (((ca,), (cb,)), ((), ())), preferred_element_type=F32)


def after(value, *others):
    return lax.optimization_barrier((value,) + others)[0]


def swap(v, step):
    name, bit, _ = STEPS[step]
    return lax.ppermute(v, name, [(i, i ^ bit) for i in range(lax.axis_size(name))])


def hold(values, *gates):
    return list(lax.optimization_barrier((*values, *gates))[: len(values)])


def reduce_step(v, step):
    dim = STEPS[step][2]
    got = swap(lax.slice_in_dim(v, 1, 2, axis=dim), step)
    return (lax.slice_in_dim(v, 0, 1, axis=dim).astype(F32) + got.astype(F32)).astype(BF)


def chain_step(parts, i):
    return [reduce_step(v, order[i]) for v, order in zip(parts, (ORDER_A, ORDER_B))]


def reduce_first(left, rights, *gates):
    half = left.shape[0] // 2
    pair, sends = [], []
    later = after(left, *gates) if gates else left
    for right in rights:
        sends.append(dot(left[half:], right, 1, 1).astype(BF))
        got = swap(sends[-1], "core")
        pair.append((dot(later[:half], right, 1, 1) + got.astype(F32)).astype(BF))
    return pair, sends


def gather_chain(parts, orders=(ORDER_A, ORDER_B), vector=None, event=None):
    rows, cols = parts[0].shape
    now = [v.reshape(1, 1, 1, 1, rows, cols) for v in parts]
    for i in range(4):
        if vector is not None:
            now = hold(now, vector)
            vector = vector + swap(vector, ORDER_A[i])
        steps = [order[3 - i] for order in orders]
        got = [swap(v, step) for v, step in zip(now, steps)]
        if i < 3:
            now = [
                jnp.concatenate([v, g], axis=STEPS[step][2])
                for v, g, step in zip(now, got, steps)
            ]
            if event is not None:
                now = event("stage%d" % i, now)
    flat_rows = [[v.reshape(8 * rows, cols) for v in pair] for pair in zip(now, got)]
    return flat_rows, vector


def whole(pairs):
    return [jnp.concatenate(pair, axis=0) for pair in pairs]


def reversed_bits(p):
    return sum(((p >> i) & 1) << (3 - i) for i in range(4))


def group_index():
    return lax.axis_index("heads") * lax.axis_size("tensor") + lax.axis_index("tensor")


def reversed_index():
    me = group_index()
    return sum(((me >> i) & 1) << (3 - i) for i in range(4))


def reorder(parts, start, dtype, tile=256, shift=None):
    rows, cols = parts[0].shape
    tile = min(tile, cols)
    per = cols // tile
    count = len(parts)
    block = rows // 16

    def kernel(at, *refs):
        out = refs[-1]
        j = pl.program_id(0)
        for i, part in enumerate(refs[:-1]):

            @pl.when(j // per == i)
            def _(part=part):
                for p in range(16):
                    src = pl.multiple_of((at[0] ^ reversed_bits(p)) * block, block)
                    out[p * block : (p + 1) * block, :] = part[pl.ds(src, block), :].astype(dtype)

    def spec(i):
        def where(j, at):
            k = jnp.clip(j - i * per, 0, per - 1)
            return (0, lax.rem(k + at[1], per))

        return pl.BlockSpec((rows, tile), where)

    at = jnp.stack([start, jnp.int32(0) if shift is None else shift // tile]).astype(jnp.int32)
    return pl.pallas_call(
        kernel,
        grid_spec=pltpu.PrefetchScalarGridSpec(
            num_scalar_prefetch=1,
            grid=(per * count,),
            in_specs=[spec(i) for i in range(count)],
            out_specs=pl.BlockSpec((rows, tile), lambda j, at: (0, j)),
        ),
        out_shape=jax.ShapeDtypeStruct((rows, cols * count), dtype),
        cost_estimate=pl.CostEstimate(
            flops=0, bytes_accessed=rows * cols * count * 8, transcendentals=0
        ),
    )(at, *parts)


VMEM_LIMIT = 48 * 2**20


def indices(shape, order):
    lead = shape[1:-1]
    spots = itertools.product(*[range(lead[i]) for i in order])
    return [tuple(spot[order.index(i)] for i in range(len(lead))) for spot in spots]


def flat(weights, orders):
    rows = min(256, weights[0].shape[0])
    spots = [indices(v.shape, order) for v, order in zip(weights, orders)]
    wide = weights[0].shape[-1]
    columns = sum(len(s) for s in spots) * wide

    def kernel(*refs):
        out, at = refs[-1], 0
        for ref, some in zip(refs, spots):
            for spot in some:
                out[:, at : at + wide] = ref[(slice(None), *spot, slice(None))].astype(BF)
                at += wide

    def spec(v):
        zeros = (0,) * (v.ndim - 1)
        return pl.BlockSpec((rows, *v.shape[1:]), lambda i: (i, *zeros))

    count = weights[0].shape[0]
    return pl.pallas_call(
        kernel,
        grid=(count // rows,),
        in_specs=[spec(v) for v in weights],
        out_specs=pl.BlockSpec((rows, columns), lambda i: (i, 0)),
        out_shape=jax.ShapeDtypeStruct((count, columns), BF),
        compiler_params=pltpu.CompilerParams(vmem_limit_bytes=VMEM_LIMIT),
        cost_estimate=pl.CostEstimate(
            flops=0, bytes_accessed=count * columns * 6, transcendentals=0
        ),
    )(*weights)


def weight_sum(left, right, got, column, shape, order, planes=False):
    rows, wide = min(256, shape[0]), shape[-1]
    tokens, columns = right.shape
    spots = indices(shape, order)
    widths = [columns] if column or len(got) == 1 else [v.shape[1] for v in got]
    homes = [(k, at) for k, w in enumerate(widths) for at in range(0, w, wide)]

    def kernel(left_ref, right_ref, *refs):
        out = refs[-1]
        total = dot(left_ref[...], right_ref[...], 0, 0)
        for j, spot in enumerate(spots):
            k, at = homes[j]
            here = refs[k][:, at : at + wide].astype(F32)
            at = (*spot, slice(None)) if planes else (slice(None), *spot)
            out[(*at, slice(None))] = total[:, j * wide : (j + 1) * wide] + here

    zeros = (0,) * (len(shape) - 1)
    block, where = (rows, *shape[1:]), lambda i: (i, *zeros)
    if planes:
        block, where = (shape[1], rows, wide), lambda i: (0, i, 0)
        shape = (shape[1], shape[0], wide)
    return pl.pallas_call(
        kernel,
        grid=(left.shape[1] // rows,),
        in_specs=[
            pl.BlockSpec((tokens, rows), lambda i: (0, i)),
            pl.BlockSpec((tokens, columns), lambda i: (0, 0)),
        ]
        + [pl.BlockSpec((rows, w), lambda i: (i, column)) for w in widths],
        out_specs=pl.BlockSpec(block, where),
        out_shape=jax.ShapeDtypeStruct(shape, F32),
        compiler_params=pltpu.CompilerParams(vmem_limit_bytes=VMEM_LIMIT),
        cost_estimate=pl.CostEstimate(
            flops=2 * tokens * left.shape[1] * columns,
            bytes_accessed=2 * left.size + 2 * right.size + 6 * left.shape[1] * columns,
            transcendentals=0,
        ),
    )(left, right, *got)


def experts(first, named, top, h, grad_part, grad_rest, weights, count):
    tokens, half = h[0].shape
    wide = weights[0].shape[1] // (3 * count)
    rows = min(1024, tokens)

    def kernel(first_ref, named_ref, ha, hb, wa, wb, part, gb, ob, act_ref, grad_ref):
        mine = (first_ref[0] + pl.program_id(0)).astype(F32)
        named = named_ref[...]
        weight = jnp.sum(
            jnp.where(named[:, :top] == mine, named[:, top : 2 * top], 0.0), 1, keepdims=True
        )
        grad = weight * (part[...] + dot(gb[...], ob[...]))
        both = dot(ha[...], wa[...]) + dot(hb[...], wb[...])
        gate, up = both[:, :wide], both[:, wide:]
        sig = 1.0 / (1.0 + jnp.exp(-gate))
        silu = gate * sig
        act_ref[...] = (weight * (silu * up)).astype(BF)
        grad_ref[:, :wide] = (grad * up * sig * (1.0 + gate * (1.0 - sig))).astype(BF)
        grad_ref[:, wide:] = (grad * silu).astype(BF)

    def by_rows(columns):
        return pl.BlockSpec((rows, columns), lambda e, r: (r, 0))

    def by_expert(columns, skip):
        return pl.BlockSpec((half, columns), lambda e, r: (0, skip + e))

    def out(columns):
        return pl.BlockSpec((rows, columns), lambda e, r: (r, e))

    return pl.pallas_call(
        kernel,
        grid=(count, tokens // rows),
        in_specs=[
            pl.BlockSpec(memory_space=pltpu.SMEM),
            by_rows(128),
            by_rows(half),
            by_rows(half),
            by_expert(2 * wide, 0),
            by_expert(2 * wide, 0),
            out(wide),
            by_rows(half),
            by_expert(wide, 2 * count),
        ],
        out_specs=[out(wide), out(2 * wide)],
        out_shape=[
            jax.ShapeDtypeStruct((tokens, count * wide), BF),
            jax.ShapeDtypeStruct((tokens, 2 * count * wide), BF),
        ],
        compiler_params=pltpu.CompilerParams(vmem_limit_bytes=VMEM_LIMIT),
        cost_estimate=pl.CostEstimate(
            flops=10 * tokens * half * count * wide,
            bytes_accessed=16 * tokens * half + 12 * half * count * wide,
            transcendentals=tokens * count * wide,
        ),
    )(first.reshape(1), named, *h, *weights, grad_part, grad_rest, weights[1])


def ordered(pairs, start, dtype, tile=512):
    rows, cols = pairs[0][0].shape
    per, block = cols // tile, rows // 8

    def kernel(at, *refs):
        out, j = refs[-1], pl.program_id(0)
        for i in range(len(pairs)):
            for top in range(2):

                @pl.when((j // per == i) & (at[0] // 8 == top))
                def _(i=i, top=top):
                    for p in range(16):
                        part = refs[2 * i + (top ^ (p & 1))]
                        src = pl.multiple_of(((at[0] ^ reversed_bits(p)) & 7) * block, block)
                        out[p * block : (p + 1) * block, :] = part[pl.ds(src, block), :].astype(
                            dtype
                        )

    def spec(i):
        return pl.BlockSpec((rows, tile), lambda j, at: (0, jnp.clip(j - i * per, 0, per - 1)))

    return pl.pallas_call(
        kernel,
        grid_spec=pltpu.PrefetchScalarGridSpec(
            num_scalar_prefetch=1,
            grid=(per * len(pairs),),
            in_specs=[spec(i) for i in range(len(pairs)) for _ in range(2)],
            out_specs=pl.BlockSpec((2 * rows, tile), lambda j, at: (0, j)),
        ),
        out_shape=jax.ShapeDtypeStruct((2 * rows, cols * len(pairs)), dtype),
        compiler_params=pltpu.CompilerParams(vmem_limit_bytes=VMEM_LIMIT),
        cost_estimate=pl.CostEstimate(
            flops=0, bytes_accessed=rows * cols * len(pairs) * 12, transcendentals=0
        ),
    )(start.reshape(1).astype(jnp.int32), *[v for pair in pairs for v in pair])


def two_way():
    return lax.axis_size("fsdp") == 2


def across(v):
    return v if v is None else lax.ppermute(v, "fsdp", [(0, 1), (1, 0)])


def spread(v, axis=0):
    if two_way():
        return v, across(v)
    full = lax.all_gather(v, "fsdp", axis=axis, tiled=True)
    half = full.shape[axis] // 2
    return (
        lax.slice_in_dim(full, 0, half, axis=axis),
        lax.slice_in_dim(full, half, 2 * half, axis=axis),
    )


def halves(v):
    half = v.shape[-1] // 2
    start = lax.axis_index("fsdp") * half if two_way() else 0
    return (
        lax.dynamic_slice_in_dim(v, start, half, v.ndim - 1),
        lax.dynamic_slice_in_dim(v, half - start, half, v.ndim - 1),
    )


def join(first, second):
    straight = jnp.concatenate([first, second], axis=-1)
    if not two_way():
        return straight
    crossed = jnp.concatenate([second, first], axis=-1)
    return jnp.where(lax.axis_index("fsdp") == 0, straight, crossed)


def partner_part(left, right):
    return dot(left[1], right, 0, 0).astype(BF)


def beside(*parts):
    return jnp.concatenate(parts, axis=1) if two_way() else None


def weight_grad(left, right, got, column, shape, order, planes=False):
    if two_way():
        total = weight_sum(left[0], right, got, column, shape, order, planes)
        return total.transpose(1, 0, 2) if planes else total
    both = jnp.concatenate([dot(part, right, 0, 0) for part in left], axis=0)
    own = lax.psum_scatter(both, "fsdp", scatter_dimension=0, tiled=True)
    lead = [shape[1 + i] for i in order]
    turned = own.reshape(shape[0], *lead, shape[-1])
    back = [1 + order.index(i) for i in range(len(order))]
    return turned.transpose(0, *back, len(shape) - 1)


def rms(first, second):
    total = jnp.sum(first * first, -1, keepdims=True) + jnp.sum(second * second, -1, keepdims=True)
    return lax.rsqrt(total / (first.shape[-1] + second.shape[-1]) + EPS)


def norm_back(grads, normed, gains, scale):
    m = [g * d for g, d in zip(gains, grads)]
    mean = (
        jnp.sum(m[0] * normed[0], -1, keepdims=True) + jnp.sum(m[1] * normed[1], -1, keepdims=True)
    ) / (m[0].shape[-1] + m[1].shape[-1])
    return [scale * (a - n * mean) for a, n in zip(m, normed)]


def local(
    tokens,
    attn_qkv,
    attn_out,
    norm_gains,
    expert_in,
    expert_out,
    segment_ids,
    keep_mask,
    routes,
    gate_weights,
    cotangent,
):
    tok_count, width = tokens.shape
    head_width = attn_qkv.shape[2]
    seq_count = tok_count // SEQ_LEN
    own_experts, hidden_width = expert_in.shape[2:]
    columns = own_experts * hidden_width
    rank, rank_reversed = group_index(), reversed_index()
    shard = tok_count // 16
    half = width // 2

    gains = [g.astype(F32) for g in spread(norm_gains.astype(BF), 1)]
    gain_one, gain_two = [g[0] for g in gains], [g[1] for g in gains]
    w_qkv = spread(attn_qkv.astype(BF).reshape(-1, 3 * head_width))
    w_o_own = after(attn_out.astype(BF).T, w_qkv[0])
    w_o = spread(w_o_own, 1)
    w_experts_own = flat([expert_in, expert_out], [(1, 0), (0,)])
    w_experts = spread(after(w_experts_own, w_o_own))
    w_in = [w[:, : 2 * columns] for w in w_experts]
    w_out = [w[:, 2 * columns :] for w in w_experts]

    x = [v.astype(F32) for v in halves(after(tokens, w_experts_own))]
    r_one = rms(*x)
    h_one = [(v * r_one * g).astype(BF) for v, g in zip(x, gain_one)]
    projected = (dot(h_one[0], w_qkv[0]) + dot(h_one[1], w_qkv[1])).astype(BF)
    w_o = w_o[0], after(w_o[1], projected)
    w_o_full = [lax.all_gather(w, GROUP, axis=0, tiled=True) for w in w_o]
    q, k, v = [
        projected[:, i * head_width : (i + 1) * head_width].reshape(seq_count, SEQ_LEN, head_width)
        for i in range(3)
    ]
    seg = segment_ids.reshape(seq_count, SEQ_LEN)
    keep = keep_mask.reshape(seq_count, SEQ_LEN)
    diagonal = jnp.arange(SEQ_LEN)[:, None] == jnp.arange(SEQ_LEN)[None, :]
    allowed = (seg[:, :, None] == seg[:, None, :]) & ((keep[:, None, :] == 1) | diagonal[None])
    score_scale = head_width ** (-0.5)
    scores = jnp.einsum("sqe,ske->sqk", q, k, preferred_element_type=F32) * score_scale
    probs = jax.nn.softmax(jnp.where(allowed, scores, -1e30), axis=-1)
    attended = jnp.einsum("sqk,ske->sqe", probs.astype(BF), v, preferred_element_type=F32)
    attended = attended.reshape(tok_count, head_width).astype(BF)

    attended_rows = lax.all_to_all(attended, GROUP, 0, 1, tiled=True)
    first_expert = lax.axis_index("heads") * own_experts
    named = jnp.concatenate([routes.astype(F32), gate_weights], axis=1)
    top = routes.shape[1]
    named = jnp.pad(named, ((0, 0), (0, 128 - 2 * top)))
    named = reorder([named], rank, F32)
    attended_rows = after(attended_rows, named)
    start = lax.axis_index("fsdp") * half if two_way() else jnp.int32(0)
    grad_out = reorder([cotangent], rank, BF, shift=start)
    attended_rows = after(attended_rows, grad_out)
    grad_out = grad_out[:, :half], grad_out[:, half:]
    grad_act_own = dot(grad_out[0], w_out[0])
    attended_rows = after(attended_rows, grad_act_own)
    x_rows = halves(lax.dynamic_slice_in_dim(tokens, rank * shard, shard, 0))
    x_rows = [v.astype(F32) for v in x_rows]
    middle = [v + dot(attended_rows, w) for v, w in zip(x_rows, w_o_full)]
    r_two = rms(*middle)
    n_two = [v * r_two for v in middle]
    h_two_rows = [(n * g).astype(BF) for n, g in zip(n_two, gain_two)]
    h_two = whole(gather_chain(h_two_rows)[0])

    act, grad_gate_up = experts(
        first_expert, named, top, h_two, grad_act_own, grad_out[1], w_experts, own_experts
    )
    done = {}

    def weight_part(left, right, begin, end):
        def make(gates):
            if not two_way() or begin == end:
                return ()
            return partner_part(left, after(right, *gates)[:, begin:end])

        return make

    def moved(name):
        return lambda gates: jax.tree.map(across, done[name])

    def mixture_step(before, i):
        return lambda gates: chain_step(hold(done[before], *gates), i)

    def mixture_sends(gates):
        left = after(act, *gates)[tok_count // 2 :]
        return [dot(left, w, 1, 1).astype(BF) for w in w_out]

    def mixture_core(gates):
        left = after(act, *gates)[: tok_count // 2]
        pair = [
            (dot(left, w, 1, 1) + swap(v, "core").astype(F32)).astype(BF)
            for w, v in zip(w_out, done["mix_send"])
        ]
        return [v.reshape(1, 2, 2, 2, shard, half) for v in pair]

    def gather_branch(gates):
        rows = jnp.concatenate(hold(grad_branch_rows, *gates), axis=1)
        return lax.all_gather(rows, GROUP, axis=0, tiled=True)

    def gather_output(gates):
        pair = [v.reshape(shard, half) for v in done["mix3"]]
        rows = join(*[(a + b.astype(F32)).astype(BF) for a, b in zip(middle, pair)])
        return lax.all_gather(after(rows, done["branch"]), GROUP, axis=0, tiled=True)

    def branch_halves():
        return done["branch"][:, :half], done["branch"][:, half:]

    def attention_parts(gates):
        if not two_way():
            return ()
        return beside(done["qkv"], partner_part(branch_halves(), attended))

    def expert_in_whole(gates):
        moves = jax.tree.leaves((done["in0_got"], done["in1_got"]))
        right = after(grad_gate_up, *gates)
        return weight_grad(h_two, right, moves, 0, expert_in.shape, (1, 0))

    def expert_out_whole(gates):
        right = after(act, *gates)
        return weight_grad(grad_out, right, [done["out_got"]], 0, expert_out.shape, (0,))

    split = 2 * columns
    make = {
        "in0": weight_part(h_two, grad_gate_up, 0, split),
        "in0_got": moved("in0"),
        "in1": weight_part(h_two, grad_gate_up, split, 2 * columns),
        "in1_got": moved("in1"),
        "out": weight_part(grad_out, act, 0, columns),
        "out_got": moved("out"),
        "mix_send": mixture_sends,
        "mix0": mixture_core,
        "mix1": mixture_step("mix0", 1),
        "mix2": mixture_step("mix1", 2),
        "mix3": mixture_step("mix2", 3),
        "branch": gather_branch,
        "output": gather_output,
        "qkv": lambda gates: partner_part(h_one, after(grad_projected, *gates)),
        "attention": attention_parts,
        "attention_got": moved("attention"),
        "in_whole": expert_in_whole,
        "out_whole": expert_out_whole,
    }

    def event(name, values):
        waits = [v for piece in PLAN["wait"].get(name, ()) for v in jax.tree.leaves(done[piece])]
        values = hold(values, *waits)
        for piece in PLAN["make"].get(name, ()):
            done[piece] = make[piece](values)
        return values

    grad_two, _ = reduce_first(grad_gate_up, w_in)
    event("core2", grad_two)
    chain = [v.reshape(1, 2, 2, 2, shard, half) for v in grad_two]
    for i, name in ((1, "two1"), (2, "two2"), (3, "two3")):
        chain = event(name, chain_step(chain, i))
    grad_two = [v.reshape(shard, half).astype(F32) for v in chain]

    out_in_rows = halves(lax.dynamic_slice_in_dim(cotangent, rank * shard, shard, 0))
    out_in_rows = [v.astype(F32) for v in out_in_rows]
    grad_middle = [
        a + b for a, b in zip(out_in_rows, norm_back(grad_two, n_two, gain_two, r_two))
    ]
    gain_two_part = join(*[jnp.sum(g * n, axis=0) for g, n in zip(grad_two, n_two)])
    grad_branch_rows = [g.astype(BF) for g in grad_middle]
    grad_attended_rows = (
        dot(grad_branch_rows[0], w_o_full[0], 1, 1) + dot(grad_branch_rows[1], w_o_full[1], 1, 1)
    ).astype(BF)
    event("do", [grad_attended_rows])
    grad_attended = lax.all_to_all(grad_attended_rows, GROUP, 1, 0, tiled=True)
    grad_attended = event("a2a", [grad_attended])[0]
    grad_attended = grad_attended.reshape(seq_count, SEQ_LEN, head_width)

    grad_v = jnp.einsum("sqk,sqe->ske", probs.astype(BF), grad_attended, preferred_element_type=F32)
    grad_probs = jnp.einsum("sqe,ske->sqk", grad_attended, v, preferred_element_type=F32)
    grad_scores = probs * (grad_probs - jnp.sum(probs * grad_probs, axis=-1, keepdims=True))
    grad_scores = grad_scores.astype(BF)
    grad_q = jnp.einsum("sqk,ske->sqe", grad_scores, k, preferred_element_type=F32) * score_scale
    grad_k = jnp.einsum("sqk,sqe->ske", grad_scores, q, preferred_element_type=F32) * score_scale
    grad_q, grad_k = event("qk", [grad_q, grad_k])
    grad_projected = jnp.concatenate([grad_q, grad_k, grad_v], axis=-1)
    grad_projected = grad_projected.reshape(tok_count, 3 * head_width).astype(BF)
    grad_projected_blocks = reorder([grad_projected], rank, BF, tile=3 * head_width)
    event("blocks", [grad_projected_blocks])
    grad_one, _ = reduce_first(grad_projected_blocks, w_qkv)
    chain = event("core1", grad_one)
    chain = [v.reshape(1, 2, 2, 2, shard, half) for v in chain]
    for i, name in ((1, "one1"), (2, "one2"), (3, "one3")):
        chain = event(name, chain_step(chain, i))
    grad_one = [v.reshape(shard, half).astype(F32) for v in chain]

    r_rows = rms(*x_rows)
    n_rows = [v * r_rows for v in x_rows]
    gain_one_part = join(*[jnp.sum(g * n, axis=0) for g, n in zip(grad_one, n_rows)])
    gain_parts = jnp.stack([gain_one_part, gain_two_part])
    grad_rows = join(
        *[a + b for a, b in zip(grad_middle, norm_back(grad_one, n_rows, gain_one, r_rows))]
    ).astype(BF)
    grad_rows = event("rows", [grad_rows])[0]
    at_stage = {}

    def noted(name, now):
        at_stage[name] = now
        return event(name, now)

    input_grad, _ = gather_chain([grad_rows[:, :half], grad_rows[:, half:]], event=noted)
    gain_parts = after(gain_parts, *at_stage["stage2"])
    for step in ORDER_A:
        gain_parts = gain_parts + swap(gain_parts, step)
    event("end", [gain_parts])

    output, expert_in_grad, expert_out_grad = done["output"], done["in_whole"], done["out_whole"]
    attention_got = [done["attention_got"]]
    qkv_grad = weight_grad(h_one, grad_projected, attention_got, 0, attn_qkv.shape, (0,), True)
    out_grad = weight_grad(branch_halves(), attended, attention_got, 3, attn_out.shape, ())
    input_grad = ordered(input_grad, rank_reversed, F32)
    if two_way():
        got = after(across(gain_parts), input_grad, qkv_grad, out_grad, expert_out_grad)
        gain_parts = gain_parts + got
    else:
        gain_parts = lax.psum(gain_parts, "fsdp")
    own_width = norm_gains.shape[1]
    gains_grad = lax.dynamic_slice_in_dim(
        gain_parts, lax.axis_index("fsdp") * own_width, own_width, 1
    )

    return (
        output,
        input_grad,
        qkv_grad,
        out_grad,
        gains_grad,
        expert_in_grad,
        expert_out_grad,
    )


def solution(mesh):
    placed = (
        P("fsdp", None),
        P("fsdp", None, ("heads", "tensor")),
        P("fsdp", ("heads", "tensor")),
        P(None, "fsdp"),
        P("fsdp", None, "heads", "tensor"),
        P("fsdp", "heads", "tensor"),
        P("fsdp"),
        P("fsdp"),
        P("fsdp", None),
        P("fsdp", None),
        P("fsdp", None),
    )
    return jax.shard_map(
        local,
        mesh=mesh,
        in_specs=placed,
        out_specs=(
            P("fsdp", None),
            P("fsdp", None),
            P("fsdp", None, ("heads", "tensor")),
            P("fsdp", ("heads", "tensor")),
            P(None, "fsdp"),
            P("fsdp", None, "heads", "tensor"),
            P("fsdp", "heads", "tensor"),
        ),
        check_vma=False,
    )
```

```python
import itertools

import jax
import jax.numpy as jnp
from jax import lax
from jax.experimental import pallas as pl
from jax.experimental.pallas import tpu as pltpu
from jax.sharding import PartitionSpec as P

SEQ_LEN = 1024
EPS = 1e-06
BF = jnp.bfloat16
F32 = jnp.float32
GROUP = ("heads", "tensor")
EVERY = ("fsdp", "heads", "tensor")

STEPS = {
    "core": ("tensor", 1, 0),
    "x": ("tensor", 2, 1),
    "z0": ("heads", 1, 2),
    "z1": ("heads", 2, 3),
}
BITS = (1, 2, 4, 8)
ORDER_A = ("core", "x", "z0", "z1")
ORDER_B = ("core", "z0", "z1", "x")


PLAN = {
    "make": {
        "core2": ("in0", "in0_got"),
        "two1": ("in1", "in1_got", "out", "out_got"),
        "two2": ("mix_send",),
        "do": ("branch", "mix0", "mix1"),
        "blocks": ("mix2",),
        "core1": ("qkv",),
        "one2": ("mix3", "in_whole", "attention", "attention_got"),
        "one3": ("output",),
        "stage1": ("out_whole",),
    },
    "wait": {
        "two1": ("in0",),
        "two2": ("out",),
        "one1": ("qkv",),
        "one2": ("in0_got",),
        "one3": ("in_whole", "mix3"),
        "stage1": ("out_got",),
        "stage2": ("output", "out_whole", "attention_got"),
    },
}


def dot(a, b, ca=1, cb=0):
    return lax.dot_general(a, b, (((ca,), (cb,)), ((), ())), preferred_element_type=F32)


def after(value, *others):
    return lax.optimization_barrier((value,) + others)[0]


def swap(v, step):
    name, bit, _ = STEPS[step]
    return lax.ppermute(v, name, [(i, i ^ bit) for i in range(lax.axis_size(name))])


def hold(values, *gates):
    return list(lax.optimization_barrier((*values, *gates))[: len(values)])


def reduce_step(v, step):
    dim = STEPS[step][2]
    got = swap(lax.slice_in_dim(v, 1, 2, axis=dim), step)
    return (lax.slice_in_dim(v, 0, 1, axis=dim).astype(F32) + got.astype(F32)).astype(BF)


def chain_step(parts, i):
    return [reduce_step(v, order[i]) for v, order in zip(parts, (ORDER_A, ORDER_B))]


def reduce_first(left, rights, *gates):
    half = left.shape[0] // 2
    pair, sends = [], []
    later = after(left, *gates) if gates else left
    for right in rights:
        sends.append(dot(left[half:], right, 1, 1).astype(BF))
        got = swap(sends[-1], "core")
        pair.append((dot(later[:half], right, 1, 1) + got.astype(F32)).astype(BF))
    return pair, sends


def gather_chain(parts, orders=(ORDER_A, ORDER_B), vector=None, event=None):
    rows, cols = parts[0].shape
    now = [v.reshape(1, 1, 1, 1, rows, cols) for v in parts]
    for i in range(4):
        if vector is not None:
            now = hold(now, vector)
            vector = vector + swap(vector, ORDER_A[i])
        steps = [order[3 - i] for order in orders]
        got = [swap(v, step) for v, step in zip(now, steps)]
        if i < 3:
            now = [
                jnp.concatenate([v, g], axis=STEPS[step][2])
                for v, g, step in zip(now, got, steps)
            ]
            if event is not None:
                now = event("stage%d" % i, now)
    flat_rows = [[v.reshape(8 * rows, cols) for v in pair] for pair in zip(now, got)]
    return flat_rows, vector


def whole(pairs):
    return [jnp.concatenate(pair, axis=0) for pair in pairs]


def reversed_bits(p):
    return sum(((p >> i) & 1) << (3 - i) for i in range(4))


def group_index():
    return lax.axis_index("heads") * lax.axis_size("tensor") + lax.axis_index("tensor")


def reversed_index():
    me = group_index()
    return sum(((me >> i) & 1) << (3 - i) for i in range(4))


def reorder(parts, start, dtype, tile=256, shift=None):
    rows, cols = parts[0].shape
    tile = min(tile, cols)
    per = cols // tile
    count = len(parts)
    block = rows // 16

    def kernel(at, *refs):
        out = refs[-1]
        j = pl.program_id(0)
        for i, part in enumerate(refs[:-1]):

            @pl.when(j // per == i)
            def _(part=part):
                for p in range(16):
                    src = pl.multiple_of((at[0] ^ reversed_bits(p)) * block, block)
                    out[p * block : (p + 1) * block, :] = part[pl.ds(src, block), :].astype(dtype)

    def spec(i):
        def where(j, at):
            k = jnp.clip(j - i * per, 0, per - 1)
            return (0, lax.rem(k + at[1], per))

        return pl.BlockSpec((rows, tile), where)

    at = jnp.stack([start, jnp.int32(0) if shift is None else shift // tile]).astype(jnp.int32)
    return pl.pallas_call(
        kernel,
        grid_spec=pltpu.PrefetchScalarGridSpec(
            num_scalar_prefetch=1,
            grid=(per * count,),
            in_specs=[spec(i) for i in range(count)],
            out_specs=pl.BlockSpec((rows, tile), lambda j, at: (0, j)),
        ),
        out_shape=jax.ShapeDtypeStruct((rows, cols * count), dtype),
        cost_estimate=pl.CostEstimate(
            flops=0, bytes_accessed=rows * cols * count * 8, transcendentals=0
        ),
    )(at, *parts)


VMEM_LIMIT = 48 * 2**20


def indices(shape, order):
    lead = shape[1:-1]
    spots = itertools.product(*[range(lead[i]) for i in order])
    return [tuple(spot[order.index(i)] for i in range(len(lead))) for spot in spots]


def flat(weights, orders):
    rows = min(128, weights[0].shape[0])
    spots = [indices(v.shape, order) for v, order in zip(weights, orders)]
    wide = weights[0].shape[-1]
    columns = sum(len(s) for s in spots) * wide

    def kernel(*refs):
        out, at = refs[-1], 0
        for ref, some in zip(refs, spots):
            for spot in some:
                out[:, at : at + wide] = ref[(slice(None), *spot, slice(None))].astype(BF)
                at += wide

    def spec(v):
        zeros = (0,) * (v.ndim - 1)
        return pl.BlockSpec((rows, *v.shape[1:]), lambda i: (i, *zeros))

    count = weights[0].shape[0]
    return pl.pallas_call(
        kernel,
        grid=(count // rows,),
        in_specs=[spec(v) for v in weights],
        out_specs=pl.BlockSpec((rows, columns), lambda i: (i, 0)),
        out_shape=jax.ShapeDtypeStruct((count, columns), BF),
        compiler_params=pltpu.CompilerParams(vmem_limit_bytes=VMEM_LIMIT),
        cost_estimate=pl.CostEstimate(
            flops=0, bytes_accessed=count * columns * 6, transcendentals=0
        ),
    )(*weights)


def weight_sum(left, right, got, column, shape, order, planes=False):
    rows, wide = min(512, shape[0]), shape[-1]
    tokens, columns = right.shape
    spots = indices(shape, order)
    widths = [columns] if column or len(got) == 1 else [v.shape[1] for v in got]
    homes = [(k, at) for k, w in enumerate(widths) for at in range(0, w, wide)]

    def kernel(left_ref, right_ref, *refs):
        out = refs[-1]
        total = dot(left_ref[...], right_ref[...], 0, 0)
        for j, spot in enumerate(spots):
            k, at = homes[j]
            here = refs[k][:, at : at + wide].astype(F32)
            at = (*spot, slice(None)) if planes else (slice(None), *spot)
            out[(*at, slice(None))] = total[:, j * wide : (j + 1) * wide] + here

    zeros = (0,) * (len(shape) - 1)
    block, where = (rows, *shape[1:]), lambda i: (i, *zeros)
    if planes:
        block, where = (shape[1], rows, wide), lambda i: (0, i, 0)
        shape = (shape[1], shape[0], wide)
    return pl.pallas_call(
        kernel,
        grid=(left.shape[1] // rows,),
        in_specs=[
            pl.BlockSpec((tokens, rows), lambda i: (0, i)),
            pl.BlockSpec((tokens, columns), lambda i: (0, 0)),
        ]
        + [pl.BlockSpec((rows, w), lambda i: (i, column)) for w in widths],
        out_specs=pl.BlockSpec(block, where),
        out_shape=jax.ShapeDtypeStruct(shape, F32),
        compiler_params=pltpu.CompilerParams(vmem_limit_bytes=VMEM_LIMIT),
        cost_estimate=pl.CostEstimate(
            flops=2 * tokens * left.shape[1] * columns,
            bytes_accessed=2 * left.size + 2 * right.size + 6 * left.shape[1] * columns,
            transcendentals=0,
        ),
    )(left, right, *got)


def experts(first, named, top, h, grad_part, grad_rest, weights, count):
    tokens, half = h[0].shape
    wide = weights[0].shape[1] // (3 * count)
    rows = min(1024, tokens)

    def kernel(first_ref, named_ref, ha, hb, wa, wb, part, gb, ob, act_ref, grad_ref):
        mine = (first_ref[0] + pl.program_id(0)).astype(F32)
        named = named_ref[...]
        weight = jnp.sum(
            jnp.where(named[:, :top] == mine, named[:, top : 2 * top], 0.0), 1, keepdims=True
        )
        grad = weight * (part[...] + dot(gb[...], ob[...]))
        both = dot(ha[...], wa[...]) + dot(hb[...], wb[...])
        gate, up = both[:, :wide], both[:, wide:]
        sig = 1.0 / (1.0 + jnp.exp(-gate))
        silu = gate * sig
        act_ref[...] = (weight * (silu * up)).astype(BF)
        grad_ref[:, :wide] = (grad * up * sig * (1.0 + gate * (1.0 - sig))).astype(BF)
        grad_ref[:, wide:] = (grad * silu).astype(BF)

    def by_rows(columns):
        return pl.BlockSpec((rows, columns), lambda e, r: (r, 0))

    def by_expert(columns, skip):
        return pl.BlockSpec((half, columns), lambda e, r: (0, skip + e))

    def out(columns):
        return pl.BlockSpec((rows, columns), lambda e, r: (r, e))

    return pl.pallas_call(
        kernel,
        grid=(count, tokens // rows),
        in_specs=[
            pl.BlockSpec(memory_space=pltpu.SMEM),
            by_rows(128),
            by_rows(half),
            by_rows(half),
            by_expert(2 * wide, 0),
            by_expert(2 * wide, 0),
            out(wide),
            by_rows(half),
            by_expert(wide, 2 * count),
        ],
        out_specs=[out(wide), out(2 * wide)],
        out_shape=[
            jax.ShapeDtypeStruct((tokens, count * wide), BF),
            jax.ShapeDtypeStruct((tokens, 2 * count * wide), BF),
        ],
        compiler_params=pltpu.CompilerParams(vmem_limit_bytes=VMEM_LIMIT),
        cost_estimate=pl.CostEstimate(
            flops=10 * tokens * half * count * wide,
            bytes_accessed=16 * tokens * half + 12 * half * count * wide,
            transcendentals=tokens * count * wide,
        ),
    )(first.reshape(1), named, *h, *weights, grad_part, grad_rest, weights[1])


def ordered(pairs, start, dtype, tile=1024):
    rows, cols = pairs[0][0].shape
    per, block = cols // tile, rows // 8

    def kernel(at, *refs):
        out, j = refs[-1], pl.program_id(0)
        for i in range(len(pairs)):
            for top in range(2):

                @pl.when((j // per == i) & (at[0] // 8 == top))
                def _(i=i, top=top):
                    for p in range(16):
                        part = refs[2 * i + (top ^ (p & 1))]
                        src = pl.multiple_of(((at[0] ^ reversed_bits(p)) & 7) * block, block)
                        out[p * block : (p + 1) * block, :] = part[pl.ds(src, block), :].astype(
                            dtype
                        )

    def spec(i):
        return pl.BlockSpec((rows, tile), lambda j, at: (0, jnp.clip(j - i * per, 0, per - 1)))

    return pl.pallas_call(
        kernel,
        grid_spec=pltpu.PrefetchScalarGridSpec(
            num_scalar_prefetch=1,
            grid=(per * len(pairs),),
            in_specs=[spec(i) for i in range(len(pairs)) for _ in range(2)],
            out_specs=pl.BlockSpec((2 * rows, tile), lambda j, at: (0, j)),
        ),
        out_shape=jax.ShapeDtypeStruct((2 * rows, cols * len(pairs)), dtype),
        compiler_params=pltpu.CompilerParams(vmem_limit_bytes=VMEM_LIMIT),
        cost_estimate=pl.CostEstimate(
            flops=0, bytes_accessed=rows * cols * len(pairs) * 12, transcendentals=0
        ),
    )(start.reshape(1).astype(jnp.int32), *[v for pair in pairs for v in pair])


def two_way():
    return lax.axis_size("fsdp") == 2


def across(v):
    return v if v is None else lax.ppermute(v, "fsdp", [(0, 1), (1, 0)])


def spread(v, axis=0):
    if two_way():
        return v, across(v)
    full = lax.all_gather(v, "fsdp", axis=axis, tiled=True)
    half = full.shape[axis] // 2
    return (
        lax.slice_in_dim(full, 0, half, axis=axis),
        lax.slice_in_dim(full, half, 2 * half, axis=axis),
    )


def halves(v):
    half = v.shape[-1] // 2
    start = lax.axis_index("fsdp") * half if two_way() else 0
    return (
        lax.dynamic_slice_in_dim(v, start, half, v.ndim - 1),
        lax.dynamic_slice_in_dim(v, half - start, half, v.ndim - 1),
    )


def join(first, second):
    straight = jnp.concatenate([first, second], axis=-1)
    if not two_way():
        return straight
    crossed = jnp.concatenate([second, first], axis=-1)
    return jnp.where(lax.axis_index("fsdp") == 0, straight, crossed)


def partner_part(left, right):
    return dot(left[1], right, 0, 0).astype(BF)


def beside(*parts):
    return jnp.concatenate(parts, axis=1) if two_way() else None


def weight_grad(left, right, got, column, shape, order, planes=False):
    if two_way():
        total = weight_sum(left[0], right, got, column, shape, order, planes)
        return total.transpose(1, 0, 2) if planes else total
    both = jnp.concatenate([dot(part, right, 0, 0) for part in left], axis=0)
    own = lax.psum_scatter(both, "fsdp", scatter_dimension=0, tiled=True)
    lead = [shape[1 + i] for i in order]
    turned = own.reshape(shape[0], *lead, shape[-1])
    back = [1 + order.index(i) for i in range(len(order))]
    return turned.transpose(0, *back, len(shape) - 1)


def rms(first, second):
    total = jnp.sum(first * first, -1, keepdims=True) + jnp.sum(second * second, -1, keepdims=True)
    return lax.rsqrt(total / (first.shape[-1] + second.shape[-1]) + EPS)


def norm_back(grads, normed, gains, scale):
    m = [g * d for g, d in zip(gains, grads)]
    mean = (
        jnp.sum(m[0] * normed[0], -1, keepdims=True) + jnp.sum(m[1] * normed[1], -1, keepdims=True)
    ) / (m[0].shape[-1] + m[1].shape[-1])
    return [scale * (a - n * mean) for a, n in zip(m, normed)]


def local(
    tokens,
    attn_qkv,
    attn_out,
    norm_gains,
    expert_in,
    expert_out,
    segment_ids,
    keep_mask,
    routes,
    gate_weights,
    cotangent,
):
    tok_count, width = tokens.shape
    head_width = attn_qkv.shape[2]
    seq_count = tok_count // SEQ_LEN
    own_experts, hidden_width = expert_in.shape[2:]
    columns = own_experts * hidden_width
    rank, rank_reversed = group_index(), reversed_index()
    shard = tok_count // 16
    half = width // 2

    gains = [g.astype(F32) for g in spread(norm_gains.astype(BF), 1)]
    gain_one, gain_two = [g[0] for g in gains], [g[1] for g in gains]
    w_qkv = spread(attn_qkv.astype(BF).reshape(-1, 3 * head_width))
    w_o_own = after(attn_out.astype(BF).T, w_qkv[0])
    w_o = spread(w_o_own, 1)
    w_experts_own = flat([expert_in, expert_out], [(1, 0), (0,)])
    w_experts = spread(after(w_experts_own, w_o_own))
    w_in = [w[:, : 2 * columns] for w in w_experts]
    w_out = [w[:, 2 * columns :] for w in w_experts]

    x = [v.astype(F32) for v in halves(after(tokens, w_experts_own))]
    r_one = rms(*x)
    h_one = [(v * r_one * g).astype(BF) for v, g in zip(x, gain_one)]
    projected = (dot(h_one[0], w_qkv[0]) + dot(h_one[1], w_qkv[1])).astype(BF)
    w_o = w_o[0], after(w_o[1], projected)
    w_o_full = [lax.all_gather(w, GROUP, axis=0, tiled=True) for w in w_o]
    q, k, v = [
        projected[:, i * head_width : (i + 1) * head_width].reshape(seq_count, SEQ_LEN, head_width)
        for i in range(3)
    ]
    seg = segment_ids.reshape(seq_count, SEQ_LEN)
    keep = keep_mask.reshape(seq_count, SEQ_LEN)
    diagonal = jnp.arange(SEQ_LEN)[:, None] == jnp.arange(SEQ_LEN)[None, :]
    allowed = (seg[:, :, None] == seg[:, None, :]) & ((keep[:, None, :] == 1) | diagonal[None])
    score_scale = head_width ** (-0.5)
    scores = jnp.einsum("sqe,ske->sqk", q, k, preferred_element_type=F32) * score_scale
    probs = jax.nn.softmax(jnp.where(allowed, scores, -1e30), axis=-1)
    attended = jnp.einsum("sqk,ske->sqe", probs.astype(BF), v, preferred_element_type=F32)
    attended = attended.reshape(tok_count, head_width).astype(BF)

    attended_rows = lax.all_to_all(attended, GROUP, 0, 1, tiled=True)
    first_expert = lax.axis_index("heads") * own_experts
    named = jnp.concatenate([routes.astype(F32), gate_weights], axis=1)
    top = routes.shape[1]
    named = jnp.pad(named, ((0, 0), (0, 128 - 2 * top)))
    named = reorder([named], rank, F32)
    attended_rows = after(attended_rows, named)
    start = lax.axis_index("fsdp") * half if two_way() else jnp.int32(0)
    grad_out = reorder([cotangent], rank, BF, shift=start)
    attended_rows = after(attended_rows, grad_out)
    grad_out = grad_out[:, :half], grad_out[:, half:]
    grad_act_own = dot(grad_out[0], w_out[0])
    attended_rows = after(attended_rows, grad_act_own)
    x_rows = halves(lax.dynamic_slice_in_dim(tokens, rank * shard, shard, 0))
    x_rows = [v.astype(F32) for v in x_rows]
    middle = [v + dot(attended_rows, w) for v, w in zip(x_rows, w_o_full)]
    r_two = rms(*middle)
    n_two = [v * r_two for v in middle]
    h_two_rows = [(n * g).astype(BF) for n, g in zip(n_two, gain_two)]
    h_two = whole(gather_chain(h_two_rows)[0])

    act, grad_gate_up = experts(
        first_expert, named, top, h_two, grad_act_own, grad_out[1], w_experts, own_experts
    )
    done = {}

    def weight_part(left, right, begin, end):
        def make(gates):
            if not two_way() or begin == end:
                return ()
            return partner_part(left, after(right, *gates)[:, begin:end])

        return make

    def moved(name):
        return lambda gates: jax.tree.map(across, done[name])

    def mixture_step(before, i):
        return lambda gates: chain_step(hold(done[before], *gates), i)

    def mixture_sends(gates):
        left = after(act, *gates)[tok_count // 2 :]
        return [dot(left, w, 1, 1).astype(BF) for w in w_out]

    def mixture_core(gates):
        left = after(act, *gates)[: tok_count // 2]
        pair = [
            (dot(left, w, 1, 1) + swap(v, "core").astype(F32)).astype(BF)
            for w, v in zip(w_out, done["mix_send"])
        ]
        return [v.reshape(1, 2, 2, 2, shard, half) for v in pair]

    def gather_branch(gates):
        rows = jnp.concatenate(hold(grad_branch_rows, *gates), axis=1)
        return lax.all_gather(rows, GROUP, axis=0, tiled=True)

    def gather_output(gates):
        pair = [v.reshape(shard, half) for v in done["mix3"]]
        rows = join(*[(a + b.astype(F32)).astype(BF) for a, b in zip(middle, pair)])
        return lax.all_gather(after(rows, done["branch"]), GROUP, axis=0, tiled=True)

    def branch_halves():
        return done["branch"][:, :half], done["branch"][:, half:]

    def attention_parts(gates):
        if not two_way():
            return ()
        return beside(done["qkv"], partner_part(branch_halves(), attended))

    def expert_in_whole(gates):
        moves = jax.tree.leaves((done["in0_got"], done["in1_got"]))
        right = after(grad_gate_up, *gates)
        return weight_grad(h_two, right, moves, 0, expert_in.shape, (1, 0))

    def expert_out_whole(gates):
        right = after(act, *gates)
        return weight_grad(grad_out, right, [done["out_got"]], 0, expert_out.shape, (0,))

    split = 2 * columns
    make = {
        "in0": weight_part(h_two, grad_gate_up, 0, split),
        "in0_got": moved("in0"),
        "in1": weight_part(h_two, grad_gate_up, split, 2 * columns),
        "in1_got": moved("in1"),
        "out": weight_part(grad_out, act, 0, columns),
        "out_got": moved("out"),
        "mix_send": mixture_sends,
        "mix0": mixture_core,
        "mix1": mixture_step("mix0", 1),
        "mix2": mixture_step("mix1", 2),
        "mix3": mixture_step("mix2", 3),
        "branch": gather_branch,
        "output": gather_output,
        "qkv": lambda gates: partner_part(h_one, after(grad_projected, *gates)),
        "attention": attention_parts,
        "attention_got": moved("attention"),
        "in_whole": expert_in_whole,
        "out_whole": expert_out_whole,
    }

    def event(name, values):
        waits = [v for piece in PLAN["wait"].get(name, ()) for v in jax.tree.leaves(done[piece])]
        values = hold(values, *waits)
        for piece in PLAN["make"].get(name, ()):
            done[piece] = make[piece](values)
        return values

    grad_two, _ = reduce_first(grad_gate_up, w_in)
    event("core2", grad_two)
    chain = [v.reshape(1, 2, 2, 2, shard, half) for v in grad_two]
    for i, name in ((1, "two1"), (2, "two2"), (3, "two3")):
        chain = event(name, chain_step(chain, i))
    grad_two = [v.reshape(shard, half).astype(F32) for v in chain]

    out_in_rows = halves(lax.dynamic_slice_in_dim(cotangent, rank * shard, shard, 0))
    out_in_rows = [v.astype(F32) for v in out_in_rows]
    grad_middle = [
        a + b for a, b in zip(out_in_rows, norm_back(grad_two, n_two, gain_two, r_two))
    ]
    gain_two_part = join(*[jnp.sum(g * n, axis=0) for g, n in zip(grad_two, n_two)])
    grad_branch_rows = [g.astype(BF) for g in grad_middle]
    grad_attended_rows = (
        dot(grad_branch_rows[0], w_o_full[0], 1, 1) + dot(grad_branch_rows[1], w_o_full[1], 1, 1)
    ).astype(BF)
    event("do", [grad_attended_rows])
    grad_attended = lax.all_to_all(grad_attended_rows, GROUP, 1, 0, tiled=True)
    grad_attended = event("a2a", [grad_attended])[0]
    grad_attended = grad_attended.reshape(seq_count, SEQ_LEN, head_width)

    grad_v = jnp.einsum("sqk,sqe->ske", probs.astype(BF), grad_attended, preferred_element_type=F32)
    grad_probs = jnp.einsum("sqe,ske->sqk", grad_attended, v, preferred_element_type=F32)
    grad_scores = probs * (grad_probs - jnp.sum(probs * grad_probs, axis=-1, keepdims=True))
    grad_scores = grad_scores.astype(BF)
    grad_q = jnp.einsum("sqk,ske->sqe", grad_scores, k, preferred_element_type=F32) * score_scale
    grad_k = jnp.einsum("sqk,sqe->ske", grad_scores, q, preferred_element_type=F32) * score_scale
    grad_q, grad_k = event("qk", [grad_q, grad_k])
    grad_projected = jnp.concatenate([grad_q, grad_k, grad_v], axis=-1)
    grad_projected = grad_projected.reshape(tok_count, 3 * head_width).astype(BF)
    grad_projected_blocks = reorder([grad_projected], rank, BF, tile=3 * head_width)
    event("blocks", [grad_projected_blocks])
    grad_one, _ = reduce_first(grad_projected_blocks, w_qkv)
    chain = event("core1", grad_one)
    chain = [v.reshape(1, 2, 2, 2, shard, half) for v in chain]
    for i, name in ((1, "one1"), (2, "one2"), (3, "one3")):
        chain = event(name, chain_step(chain, i))
    grad_one = [v.reshape(shard, half).astype(F32) for v in chain]

    r_rows = rms(*x_rows)
    n_rows = [v * r_rows for v in x_rows]
    gain_one_part = join(*[jnp.sum(g * n, axis=0) for g, n in zip(grad_one, n_rows)])
    gain_parts = jnp.stack([gain_one_part, gain_two_part])
    grad_rows = join(
        *[a + b for a, b in zip(grad_middle, norm_back(grad_one, n_rows, gain_one, r_rows))]
    ).astype(BF)
    grad_rows = event("rows", [grad_rows])[0]
    at_stage = {}

    def noted(name, now):
        at_stage[name] = now
        return event(name, now)

    input_grad, _ = gather_chain([grad_rows[:, :half], grad_rows[:, half:]], event=noted)
    gain_parts = after(gain_parts, *at_stage["stage2"])
    for step in ORDER_A:
        gain_parts = gain_parts + swap(gain_parts, step)
    event("end", [gain_parts])

    output, expert_in_grad, expert_out_grad = done["output"], done["in_whole"], done["out_whole"]
    attention_got = [done["attention_got"]]
    qkv_grad = weight_grad(h_one, grad_projected, attention_got, 0, attn_qkv.shape, (0,), True)
    out_grad = weight_grad(branch_halves(), attended, attention_got, 3, attn_out.shape, ())
    input_grad = ordered(input_grad, rank_reversed, F32)
    if two_way():
        got = after(across(gain_parts), input_grad, qkv_grad, out_grad, expert_out_grad)
        gain_parts = gain_parts + got
    else:
        gain_parts = lax.psum(gain_parts, "fsdp")
    own_width = norm_gains.shape[1]
    gains_grad = lax.dynamic_slice_in_dim(
        gain_parts, lax.axis_index("fsdp") * own_width, own_width, 1
    )

    return (
        output,
        input_grad,
        qkv_grad,
        out_grad,
        gains_grad,
        expert_in_grad,
        expert_out_grad,
    )


def solution(mesh):
    placed = (
        P("fsdp", None),
        P("fsdp", None, ("heads", "tensor")),
        P("fsdp", ("heads", "tensor")),
        P(None, "fsdp"),
        P("fsdp", None, "heads", "tensor"),
        P("fsdp", "heads", "tensor"),
        P("fsdp"),
        P("fsdp"),
        P("fsdp", None),
        P("fsdp", None),
        P("fsdp", None),
    )
    return jax.shard_map(
        local,
        mesh=mesh,
        in_specs=placed,
        out_specs=(
            P("fsdp", None),
            P("fsdp", None),
            P("fsdp", None, ("heads", "tensor")),
            P("fsdp", ("heads", "tensor")),
            P(None, "fsdp"),
            P("fsdp", None, "heads", "tensor"),
            P("fsdp", "heads", "tensor"),
        ),
        check_vma=False,
    )
```
